256 devices in a mesh: row: 8 (over z_lo, x), col: 4 (over z_hi), depth: 8 (over y, core).
Axes of the slice: x: 4, y: 4, z: 8 (z_hi: 4, z_lo: 2; z = z_hi * 2 + z_lo), core: 2. Of those that a mesh axis runs over, the one named last changes fastest.
Arguments:
- tokens: bfloat16 [8192, 5120], P(('row', 'depth'), 'col'), may hold values from -6 to 6
- bucket_ids: int32 [8192], P(('row', 'depth')), may hold values from 0 to 15
- clip_lengths: int32 [64], replicated, may hold values from 1 to 256, 8192 in all
- shift_table: float32 [16, 5120], replicated, may hold values from -3 to 3
- scale_table: float32 [16, 5120], replicated, may hold values from -2.5 to 2.5
- gate_table: float32 [16, 5120], P(None, 'col'), may hold values from 0.5 to 1.5
- w_qkv: bfloat16 [5120, 7680], P('row', 'col'), may hold values from -0.078125 to 0.078125
- q_gain: float32 [2560], P('col'), may hold values from 0.5 to 1.5
- k_gain: float32 [2560], P('col'), may hold values from 0.5 to 1.5
- w_out: bfloat16 [2560, 5120], P('row', 'col'), may hold values from -0.125 to 0.125
Outputs:
- update: bfloat16 [8192, 5120], P(('row', 'depth'), 'col')
The draws below stay inside these ranges and needn't reach their ends.
Inputs may be any that keep to these rules, and one draw needn't show every extreme that they name: `clip_lengths`: clip lengths in slab order; they sum to 8192.
All inputs are finite; a program needn't handle non-finite values.
Results may differ from the reference program's by a relative error of at most 0.0081.
Values may be sent and summed in bfloat16 or wider, within the bound.
A program may use at most 128 MiB of HBM per device.

```python
import math
import jax
import jax.numpy as jnp
import numpy as np
from jax import lax

D = 5120
HD = 128
HEADS = 20
BUCKETS = 16
FRAME = 128
CLIP_MOST = 256
TOK_DEV = 128
TOKENS = 8192
CLIPS = 64


def with_ends(values, own_key, low, largest):
    index_at = [jax.random.randint(jax.random.fold_in(own_key, axis), (), 0, length) for axis, length in enumerate(values.shape)]
    main_axis = values.shape.index(max(values.shape))
    next_to = index_at[:main_axis] + [(index_at[main_axis] + 1) % values.shape[main_axis]] + index_at[main_axis + 1:]
    return values.at[tuple(index_at)].set(low).at[tuple(next_to)].set(largest)


def levels(key, dims, pieces, smallest, top_value):
    def one(dim, shards_of):
        heights = jax.random.uniform(jax.random.fold_in(jax.random.fold_in(key, 6), dim), (shards_of,), jnp.float32, smallest / len(pieces), top_value / len(pieces))
        return jnp.repeat(jnp.exp(heights), dims[dim] // shards_of).reshape((-1,) + (1,) * (len(dims) - dim - 1))

    gain = one(*pieces[0])
    for cut in pieces[1:]:
        gain = gain * one(*cut)
    return gain


def length_profile(number_of, total, most, lean):
    weights = [(1 << 20) // math.isqrt(rank ** lean) + 1 for rank in range(2, number_of + 1)]
    surplus, counts = total - most - (number_of - 1), [1] * (number_of - 1)
    while surplus > 0:
        free = [i for i in range(number_of - 1) if counts[i] < most]
        pool, remaining = sum([weights[i] for i in free]), surplus
        for i in free:
            addition = min(most - counts[i], max(1, remaining * weights[i] // pool), surplus)
            counts[i] = counts[i] + addition
            surplus = surplus - addition
    return np.array([most] + counts)


def ragged(rng, count, total, bound, skew):
    if count == 2:
        one = jax.random.randint(rng, (), max(1, total - bound), min(bound, total - 1) + 1)
        return jnp.stack([one, total - one])
    sizes = jnp.asarray(length_profile(count, total, bound, skew), jnp.int32)
    pairs = (count - 1) // 2
    donor, receiver = sizes[1:1 + 2 * pairs:2], sizes[2:2 + 2 * pairs:2]
    margin = jnp.minimum(donor - 1, bound - receiver)
    moved = jax.random.randint(jax.random.fold_in(rng, 1), (pairs,), 0, 1 << 20) % (margin + 1)
    sizes = sizes.at[1:1 + 2 * pairs:2].set(donor - moved).at[2:2 + 2 * pairs:2].set(receiver + moved)
    return sizes[jax.random.permutation(jax.random.fold_in(rng, 2), count)]


def gaussian(stream_key, dims, width, reach, split=(), held_as=jnp.bfloat16):
    level = levels(stream_key, dims, split, -0.22, 0.18) if split else 1.0
    array = jax.random.normal(stream_key, dims, jnp.float32) * width * level
    return jnp.minimum(jnp.maximum(array, -reach), reach).astype(held_as)


def setup_inputs(seed: int = 0) -> dict:
    seeds = jax.random.split(jax.random.key(seed), 11)
    tokens = gaussian(seeds[0], (TOKENS, D), 1.0, 6.0, ((0, 64), (1, 4)))
    bucket_ids = with_ends(jax.random.randint(seeds[1], (TOKENS,), 0, BUCKETS), jax.random.fold_in(seeds[1], 1), 0, BUCKETS - 1).astype(jnp.int32)
    clip_lengths = ragged(seeds[2], CLIPS, TOKENS, CLIP_MOST, 0).astype(jnp.int32)
    shift_table = gaussian(seeds[3], (BUCKETS, D), 0.5, 3.0, (), jnp.float32)
    scale_table = gaussian(seeds[4], (BUCKETS, D), 0.4, 2.5, (), jnp.float32)
    gate_table = jnp.clip(0.5 + 1.0 * jax.random.uniform(seeds[5], (BUCKETS, D), jnp.float32) ** levels(seeds[5], (BUCKETS, D), ((1, 4),), -0.2, 0.2), 0.5, 1.5)
    w_qkv = gaussian(seeds[6], (D, 3 * HEADS * HD), D ** -0.5, 0.078125, ((0, 8), (1, 4)))
    q_gain = jnp.clip(1.0 + 0.1 * jax.random.normal(seeds[7], (HEADS * HD,), jnp.float32), 0.5, 1.5)
    k_gain = jnp.clip(1.0 + 0.1 * jax.random.normal(seeds[8], (HEADS * HD,), jnp.float32), 0.5, 1.5)
    w_out = gaussian(seeds[9], (HEADS * HD, D), (HEADS * HD) ** -0.5, 0.125, ((0, 8), (1, 4)))
    return {"tokens": tokens, "bucket_ids": bucket_ids, "clip_lengths": clip_lengths, "shift_table": shift_table, "scale_table": scale_table, "gate_table": gate_table, "w_qkv": w_qkv, "q_gain": q_gain, "k_gain": k_gain, "w_out": w_out}


eps_norm = 1e-06

def clip_places(first_row, row_count, clip_lengths):
    clip_ends = jnp.cumsum(clip_lengths, dtype=jnp.int32)
    token_index = first_row + jnp.arange(row_count, dtype=jnp.int32)
    passed = clip_ends[None, :] <= token_index[:, None]
    clip_number = lax.optimization_barrier(jnp.sum(passed.astype(jnp.int32), axis=1, dtype=jnp.int32))
    clip_start = lax.optimization_barrier(jnp.sum(jnp.where(passed, clip_lengths[None, :], 0), axis=1, dtype=jnp.int32))
    return (clip_number, token_index - clip_start)

def layer_norm(values):
    row_mean = lax.optimization_barrier(jnp.mean(values, axis=-1, keepdims=True))
    centred = values - row_mean
    spread = lax.optimization_barrier(jnp.mean(centred * centred, axis=-1, keepdims=True))
    return centred * lax.rsqrt(spread + eps_norm)

def head_norm(vectors, gains):
    power = lax.optimization_barrier(jnp.mean(vectors * vectors, axis=-1, keepdims=True))
    return vectors * lax.rsqrt(power + eps_norm) * gains

def rotary(vectors, position):
    half_width = vectors.shape[-1] // 2
    inverse = 10000.0 ** (-jnp.arange(half_width, dtype=jnp.float32) / half_width)
    angles = position.astype(jnp.float32)[:, None] * inverse[None, :]
    cosine = jnp.cos(angles)[:, None, :]
    sine = jnp.sin(angles)[:, None, :]
    front = vectors[..., :half_width]
    back = vectors[..., half_width:]
    return jnp.concatenate([front * cosine - back * sine, back * cosine + front * sine], axis=-1)

def frame_attention(queries, keys_rot, values_new, clip_number, frame_len):
    tok_rows, heads_here, head_dim = queries.shape
    frames = tok_rows // frame_len
    frame_shape = (frames, frame_len, heads_here, head_dim)
    scores = jnp.einsum('fqhd,fkhd->fhqk', queries.reshape(frame_shape).astype(jnp.float32), keys_rot.reshape(frame_shape).astype(jnp.float32)) / math.sqrt(head_dim)
    same_clip = clip_number.reshape(frames, frame_len)
    allowed = same_clip[:, None, :, None] == same_clip[:, None, None, :]
    raised = jnp.where(allowed, jnp.exp(scores), 0.0)
    weights = (raised / lax.optimization_barrier(jnp.sum(raised, axis=-1, keepdims=True))).astype(jnp.bfloat16)
    attended = jnp.einsum('fhqk,fkhd->fqhd', weights.astype(jnp.float32), values_new.reshape(frame_shape).astype(jnp.float32))
    return attended.reshape(tok_rows, heads_here * head_dim).astype(jnp.bfloat16)

def reference(tokens, bucket_ids, clip_lengths, shift_table, scale_table, gate_table, w_qkv, q_gain, k_gain, w_out):
    blocks = TOKENS // TOK_DEV

    def one_block(inputs):
        block_tokens, block_ids, block_index = inputs
        first_row = block_index * TOK_DEV
        clip_number, position = clip_places(first_row, TOK_DEV, clip_lengths)
        normed = layer_norm(block_tokens.astype(jnp.float32))
        modulated = (normed * (1.0 + scale_table[block_ids]) + shift_table[block_ids]).astype(jnp.bfloat16)
        joined = jnp.dot(modulated, w_qkv, preferred_element_type=jnp.float32).reshape(TOK_DEV, HEADS, 3, HD)
        queries = rotary(head_norm(joined[:, :, 0], q_gain.reshape(HEADS, HD)), position).astype(jnp.bfloat16)
        keys_rot = rotary(head_norm(joined[:, :, 1], k_gain.reshape(HEADS, HD)), position).astype(jnp.bfloat16)
        values_new = joined[:, :, 2].astype(jnp.bfloat16)
        attended = frame_attention(queries, keys_rot, values_new, clip_number, FRAME)
        projected = jnp.dot(attended, w_out, preferred_element_type=jnp.float32)
        return (gate_table[block_ids] * projected).astype(jnp.bfloat16)
    outputs = lax.map(one_block, (tokens.reshape(blocks, TOK_DEV, D), bucket_ids.reshape(blocks, TOK_DEV), jnp.arange(blocks, dtype=jnp.int32)))
    return outputs.reshape(TOKENS, D)
```

```python
import math

import jax
import jax.numpy as jnp
from jax import lax
from jax.experimental import pallas as pl
from jax.experimental.pallas import tpu as pltpu
from jax.sharding import PartitionSpec as P

HD = 128
EPS = 1e-06
MESH = pl.DeviceIdType.MESH


def clip_places(first_row, row_count, clip_lengths):
    clip_ends = jnp.cumsum(clip_lengths, dtype=jnp.int32)
    token_index = first_row + jnp.arange(row_count, dtype=jnp.int32)
    passed = clip_ends[None, :] <= token_index[:, None]
    clip_number = jnp.sum(passed.astype(jnp.int32), axis=1, dtype=jnp.int32)
    clip_start = jnp.sum(jnp.where(passed, clip_lengths[None, :], 0), axis=1, dtype=jnp.int32)
    return (clip_number, token_index - clip_start)


def remote(src, dst, send, recv, device):
    return pltpu.make_async_remote_copy(
        src_ref=src, dst_ref=dst, send_sem=send, recv_sem=recv, device_id=device, device_id_type=MESH
    )


class Place:
    def __init__(self):
        row = lax.axis_index("row")
        depth = lax.axis_index("depth")
        self.zh = lax.axis_index("col")
        self.zl = row // 4
        self.x = row % 4
        self.y = depth // 2
        self.core = depth % 2
        self.z = self.zh * 2 + self.zl

    def at(self, x=None, y=None, z=None, core=None):
        x = self.x if x is None else x % 4
        y = self.y if y is None else y % 4
        z = self.z if z is None else z % 8
        core = self.core if core is None else core
        return ((z % 2) * 4 + x, z // 2, y * 2 + core)


class Weights:
    def __init__(self, at, tile, buf, sems, by_columns):
        self.at, self.tile, self.buf, self.by_columns = at, tile, buf, by_columns
        self.rows, self.cols = tile.shape
        (self.sx, self.rx, self.sf, self.rf, self.sy, self.ry, self.sc, self.rc, self.own) = sems

    def cut(self, ref, first, quarter, core):
        quarter_rows = self.rows // 4
        if self.by_columns:
            half = self.cols // 2
            return ref.at[
                pl.ds(pl.multiple_of(first + quarter * quarter_rows, 16), quarter_rows),
                pl.ds(pl.multiple_of(core * half, 128), half),
            ]
        half = quarter_rows // 2
        return ref.at[pl.ds(pl.multiple_of(first + quarter * quarter_rows + core * half, 16), half), :]

    def slot(self, x, quarter, core=None):
        core = self.at.core if core is None else core
        return self.cut(self.buf, (x % 4) * self.rows, quarter % 4, core)

    def x1(self, side, i):
        a = self.at
        to = a.x + 1 if side == 0 else a.x - 1
        return remote(
            self.cut(self.tile, 0, (a.y + i) % 4, a.core),
            self.slot(a.x, a.y + i),
            self.sx.at[side, i],
            self.rx.at[side, i],
            a.at(x=to),
        )

    def x2(self, side):
        a = self.at
        frm = a.x - 1 if side == 0 else a.x + 1
        to = a.x + 1 if side == 0 else a.x - 1
        ref = self.slot(frm, a.y + side)
        return remote(ref, ref, self.sf.at[side], self.rf.at[side], a.at(x=to))

    def y1(self, t, side):
        a = self.at
        ref = self.slot(a.x + t, a.y + side)
        to = a.y + 1 if side == 0 else a.y - 1
        return remote(ref, ref, self.sy.at[t - 1, side], self.ry.at[t - 1, side], a.at(y=to))

    def c1(self, t, i):
        a = self.at
        ref = self.slot(a.x + t, a.y + i)
        return remote(ref, ref, self.sc.at[t - 1, i], self.rc.at[t - 1, i], a.at(core=1 - a.core))

    def local(self):
        first = pl.multiple_of(self.at.x * self.rows, 16)
        return pltpu.make_async_copy(self.tile, self.buf.at[pl.ds(first, self.rows), :], self.own)

    def start(self):
        for side, i in ((0, 0), (1, 1), (0, 1), (1, 0)):
            self.x1(side, i).start()
        self.local().start()

    def near(self):
        for side in (0, 1):
            t = 3 if side == 0 else 1
            self.x1(side, side).wait_recv()
            self.x2(side).start()
            self.y1(t, side).start()
            self.c1(t, side).start()
        for side in (0, 1):
            t = 3 if side == 0 else 1
            self.x1(side, 1 - side).wait_recv()
            self.y1(t, 1 - side).start()
            self.c1(t, 1 - side).start()

    def far(self):
        for side in (0, 1):
            self.x2(side).wait_recv()
            self.y1(2, side).start()
            self.c1(2, side).start()

    def across(self):
        for t in (3, 1, 2):
            for side in (0, 1):
                self.y1(t, side).wait_recv()
                self.c1(t, 3 if side == 0 else 2).start()

    def ready(self):
        self.local().wait()
        for t in (3, 1, 2):
            for i in range(4):
                self.c1(t, i).wait_recv()

    def drain(self):
        for side in (0, 1):
            for i in (0, 1):
                self.x1(side, i).wait_send()
            self.x2(side).wait_send()
        for t in (1, 2, 3):
            for side in (0, 1):
                self.y1(t, side).wait_send()
            for i in range(4):
                self.c1(t, i).wait_send()


class Spread:
    def __init__(self, at, src, buf, sems):
        self.at, self.src, self.buf = at, src, buf
        self.width = src.shape[1]
        self.send, self.recv, self.relay_send = sems

    def view(self, slot, half):
        column = pl.multiple_of((slot // 2) * self.width, 128)
        return self.buf.at[slot % 2, pl.ds(half * 64, 64), pl.ds(column, self.width)]

    def out(self, o, half):
        a = self.at
        slot = a.z % 4
        to = 2 * ((a.z // 2 + o) % 4) + a.z // 4
        return remote(
            self.src.at[pl.ds(half * 64, 64), :],
            self.view(slot, half),
            self.send.at[o, half],
            self.recv.at[slot, half],
            a.at(z=to),
        )

    def keep(self, half):
        slot = self.at.z % 4
        return pltpu.make_async_copy(
            self.src.at[pl.ds(half * 64, 64), :], self.view(slot, half), self.recv.at[slot, half]
        )

    def came(self, slot, half):
        ref = self.view(slot, half)
        pltpu.make_async_copy(ref, ref, self.recv.at[slot, half]).wait()

    def forward(self, m, half):
        a = self.at
        slot = a.z % 2 + 2 * m
        ref = self.view(slot, half)
        to = a.z + 2 if half == 0 else a.z - 2
        return remote(ref, ref, self.relay_send.at[m], self.recv.at[slot, half], a.at(z=to))

    def on_ring(self):
        return self.at.z % 2 == self.at.z // 4

    def relation(self, m):
        a = self.at
        return (a.z // 2 - (2 * (a.z % 2) + m) + 4) % 4

    def start(self):
        for o in (1, 3):
            for half in (0, 1):
                self.out(o, half).start()

        @pl.when(self.on_ring())
        def _():
            for half in (0, 1):
                self.keep(half).start()

        @pl.when(jnp.logical_not(self.on_ring()))
        def _():
            for o in (0, 2):
                for half in (0, 1):
                    self.out(o, half).start()

    def relay(self):
        for m in (0, 1):
            rel = self.relation(m)
            slot = self.at.z % 2 + 2 * m

            @pl.when(rel == 1)
            def _():
                self.came(slot, 0)
                self.forward(m, 0).start()

            @pl.when(rel == 3)
            def _():
                self.came(slot, 1)
                self.forward(m, 1).start()

    def ready(self):
        for m in (0, 1):
            rel = self.relation(m)
            slot = self.at.z % 2 + 2 * m

            @pl.when(rel != 1)
            def _():
                self.came(slot, 0)

            @pl.when(rel != 3)
            def _():
                self.came(slot, 1)

            other = 1 - self.at.z % 2 + 2 * m
            self.came(other, 0)
            self.came(other, 1)

    def drain(self):
        for o in (1, 3):
            for half in (0, 1):
                self.out(o, half).wait_send()

        @pl.when(jnp.logical_not(self.on_ring()))
        def _():
            for o in (0, 2):
                for half in (0, 1):
                    self.out(o, half).wait_send()

        for m in (0, 1):
            rel = self.relation(m)

            @pl.when(rel == 1)
            def _():
                self.forward(m, 0).wait_send()

            @pl.when(rel == 3)
            def _():
                self.forward(m, 1).wait_send()


def block_kernel(
    tokens, ids, shift, scale, gate, wq, wo, qg, kg, cosine, sine, mask, out,
    wq_all, wo_all, mod, a1, att, a2, row_a, row_b, stat_in, stat_col, stats,
    home1, mine1, theirs1, home2, mine2, theirs2, acc1, acc2,
    stat_send, stat_recv, c1_send, c1_recv, c2_send, c2_recv,
    qs0, qs1, qs2, qs3, qs4, qs5, qs6, qs7, qs8,
    os0, os1, os2, os3, os4, os5, os6, os7, os8,
    as0, as1, as2, bs0, bs1, bs2,
):
    at = Place()
    wide = tokens.shape[1]
    heads = qg.shape[0]
    buckets = shift.shape[0]

    barrier = pltpu.get_barrier_semaphore()
    friends = [at.at(z=at.z + o) for o in range(1, 8)]
    friends += [at.at(x=at.x + 1), at.at(x=at.x + 3), at.at(y=at.y + 1), at.at(y=at.y + 3)]
    friends += [at.at(core=1 - at.core)]
    for friend in friends:
        pl.semaphore_signal(barrier, inc=1, device_id=friend, device_id_type=MESH)
    pl.semaphore_wait(barrier, len(friends))

    qkv = Weights(at, wq, wq_all, (qs0, qs1, qs2, qs3, qs4, qs5, qs6, qs7, qs8), False)
    proj = Weights(at, wo, wo_all, (os0, os1, os2, os3, os4, os5, os6, os7, os8), True)
    one = Spread(at, mod, a1, (as0, as1, as2))
    two = Spread(at, att, a2, (bs0, bs1, bs2))

    qkv.start()

    lane = lax.broadcasted_iota(jnp.int32, (16, HD), 1)

    @pl.loop(0, 8)
    def _(i):
        rows = pl.ds(pl.multiple_of(i * 16, 16), 16)
        part = tokens[rows, :].astype(jnp.float32)
        mean = jnp.sum(part, axis=1, keepdims=True) * (1.0 / wide)
        part = part - mean
        spread = jnp.sum(part * part, axis=1, keepdims=True)
        stat_in[rows, :] = jnp.where(lane == 0, mean, jnp.where(lane == 1, spread, 0.0))

    stats[at.zh] = stat_in[...].T[0:8, :]

    def stat_copy(o):
        ref = stats.at[at.zh]
        return remote(ref, ref, stat_send.at[o - 1], stat_recv.at[o - 1], at.at(z=at.z + 2 * o))

    for o in (1, 3, 2):
        stat_copy(o).start()

    one_hot = (ids[...] == lax.broadcasted_iota(jnp.int32, (HD, buckets), 1)).astype(jnp.float32)
    here = pl.ds(pl.multiple_of(at.zh * wide, 128), wide)
    row_a[...] = 1.0 + jnp.dot(
        one_hot, scale[:, here], precision=lax.Precision.HIGHEST, preferred_element_type=jnp.float32
    )
    row_b[...] = jnp.dot(
        one_hot, shift[:, here], precision=lax.Precision.HIGHEST, preferred_element_type=jnp.float32
    )

    for o in (1, 3, 2):
        stat_copy(o).wait_recv()
    means = [stats[c][0:1, :] for c in range(4)]
    mean = (means[0] + means[1] + means[2] + means[3]) * 0.25
    total = jnp.zeros_like(mean)
    for c in range(4):
        apart = means[c] - mean
        total = total + stats[c][1:2, :] + wide * (apart * apart)
    rstd = lax.rsqrt(total * (1.0 / (4 * wide)) + EPS)
    index = lax.broadcasted_iota(jnp.int32, (HD, HD), 0)
    stat_col[...] = jnp.where(index == 0, mean, jnp.where(index == 1, rstd, 0.0)).T

    @pl.loop(0, 8)
    def _(i):
        rows = pl.ds(pl.multiple_of(i * 16, 16), 16)
        normed = (tokens[rows, :].astype(jnp.float32) - stat_col[rows, 0:1]) * stat_col[rows, 1:2]
        mod[rows, :] = (normed * row_a[rows, :] + row_b[rows, :]).astype(jnp.bfloat16)

    one.start()
    qkv.near()
    proj.start()
    qkv.far()
    one.relay()
    qkv.across()
    proj.near()
    proj.far()
    row_a[...] = jnp.dot(
        one_hot, gate[...], precision=lax.Precision.HIGHEST, preferred_element_type=jnp.float32
    )
    qkv.ready()
    one.ready()

    partner = at.at(z=at.zh * 2 + 1 - at.zl)
    own_rows = pl.ds(pl.multiple_of(at.zl * HD, HD), HD)
    other_rows = pl.ds(pl.multiple_of((1 - at.zl) * HD, HD), HD)

    def swap1(h):
        return remote(mine1.at[h], theirs1.at[h], c1_send.at[h], c1_recv.at[h], partner)

    def swap2(h):
        return remote(mine2.at[h], theirs2.at[h], c2_send.at[h], c2_recv.at[h], partner)

    @pl.loop(0, heads)
    def _(h):
        columns = pl.ds(pl.multiple_of(h * (3 * HD), HD), 3 * HD)
        left = a1[...].reshape(2 * HD, a1.shape[2])
        acc1[...] = jnp.dot(left, wq_all[:, columns], preferred_element_type=jnp.float32)
        mine1[h] = acc1[other_rows, :].astype(jnp.bfloat16)
        swap1(h).start()
        home1[h] = acc1[own_rows, :]

    proj.across()

    def rotate(vectors, gains):
        power = jnp.mean(vectors * vectors, axis=-1, keepdims=True)
        vectors = vectors * lax.rsqrt(power + EPS) * gains
        turned = pltpu.roll(vectors, HD // 2, axis=1)
        return (vectors * cosine[...] + turned * sine[...]).astype(jnp.bfloat16)

    @pl.loop(0, heads)
    def _(h):
        swap1(h).wait_recv()
        joined = home1[h] + theirs1[h].astype(jnp.float32)
        query = rotate(joined[:, 0:HD], qg[pl.ds(h, 1), :])
        key = rotate(joined[:, HD : 2 * HD], kg[pl.ds(h, 1), :])
        value = joined[:, 2 * HD : 3 * HD].astype(jnp.bfloat16)
        scores = lax.dot_general(
            query, key, (((1,), (1,)), ((), ())), preferred_element_type=jnp.float32
        ) * (1.0 / math.sqrt(HD))
        raised = jnp.where(mask[...] > 0.0, jnp.exp(scores), 0.0)
        weights = (raised / jnp.sum(raised, axis=-1, keepdims=True)).astype(jnp.bfloat16)
        columns = pl.ds(pl.multiple_of(h * HD, HD), HD)
        att[:, columns] = jnp.dot(weights, value, preferred_element_type=jnp.float32).astype(
            jnp.bfloat16
        )

    two.start()
    proj.ready()
    two.relay()
    two.ready()

    pieces, piece = home2.shape[0], home2.shape[2]

    @pl.loop(0, pieces)
    def _(n):
        columns = pl.ds(pl.multiple_of(n * piece, HD), piece)
        left = a2[...].reshape(2 * HD, a2.shape[2])
        acc2[...] = jnp.dot(left, wo_all[:, columns], preferred_element_type=jnp.float32)
        mine2[n] = acc2[other_rows, :].astype(jnp.bfloat16)
        swap2(n).start()
        home2[n] = acc2[own_rows, :]

    qkv.drain()
    proj.drain()
    one.drain()
    two.drain()
    for o in (1, 2, 3):
        stat_copy(o).wait_send()

    @pl.loop(0, heads)
    def _(h):
        swap1(h).wait_send()

    @pl.loop(0, pieces)
    def _(n):
        columns = pl.ds(pl.multiple_of(n * piece, HD), piece)
        swap2(n).wait_recv()
        projected = home2[n] + theirs2[n].astype(jnp.float32)
        out[:, columns] = (row_a[:, columns] * projected).astype(jnp.bfloat16)

    @pl.loop(0, pieces)
    def _(n):
        swap2(n).wait_send()


def shards(
    tokens, bucket_ids, clip_lengths, shift_table, scale_table, gate_table, w_qkv, q_gain, k_gain, w_out
):
    rows, wide = tokens.shape
    heads = w_qkv.shape[1] // (3 * HD)
    first_row = lax.axis_index(("row", "depth")) * rows
    clip_number, position = clip_places(first_row, rows, clip_lengths)
    half = HD // 2
    inverse = 10000.0 ** (-jnp.arange(half, dtype=jnp.float32) / half)
    angles = position.astype(jnp.float32)[:, None] * inverse[None, :]
    cosine, sine = jnp.cos(angles), jnp.sin(angles)
    cosine = jnp.concatenate([cosine, cosine], axis=1)
    sine = jnp.concatenate([-sine, sine], axis=1)
    mask = (clip_number[:, None] == clip_number[None, :]).astype(jnp.float32)

    pieces = 5
    piece = wide // pieces
    bf16, f32 = jnp.bfloat16, jnp.float32
    dma = pltpu.SemaphoreType.DMA
    weight_sems = [dma((2, 2)), dma((2, 2)), dma((2,)), dma((2,)), dma((3, 2)), dma((3, 2)), dma((3, 4)), dma((3, 4)), dma]
    spread_sems = [dma((4, 2)), dma((4, 2)), dma((2,))]
    vmem = pl.BlockSpec(memory_space=pltpu.VMEM)
    hbm = pl.BlockSpec(memory_space=pl.ANY)
    return pl.pallas_call(
        block_kernel,
        out_shape=jax.ShapeDtypeStruct((rows, wide), bf16),
        in_specs=[vmem] * 5 + [hbm] * 2 + [vmem] * 5,
        out_specs=vmem,
        scratch_shapes=[
            pltpu.VMEM((4 * w_qkv.shape[0], w_qkv.shape[1]), bf16),
            pltpu.VMEM((4 * w_out.shape[0], w_out.shape[1]), bf16),
            pltpu.VMEM((rows, wide), bf16),
            pltpu.VMEM((2, rows, 2 * wide), bf16),
            pltpu.VMEM((rows, heads * HD), bf16),
            pltpu.VMEM((2, rows, 2 * heads * HD), bf16),
            pltpu.VMEM((rows, wide), f32),
            pltpu.VMEM((rows, wide), f32),
            pltpu.VMEM((rows, HD), f32),
            pltpu.VMEM((rows, HD), f32),
            pltpu.VMEM((4, 8, rows), f32),
            pltpu.VMEM((heads, rows, 3 * HD), f32),
            pltpu.VMEM((heads, rows, 3 * HD), bf16),
            pltpu.VMEM((heads, rows, 3 * HD), bf16),
            pltpu.VMEM((pieces, rows, piece), f32),
            pltpu.VMEM((pieces, rows, piece), bf16),
            pltpu.VMEM((pieces, rows, piece), bf16),
            pltpu.VMEM((2 * rows, 3 * HD), f32),
            pltpu.VMEM((2 * rows, piece), f32),
            dma((3,)), dma((3,)),
            dma((heads,)), dma((heads,)),
            dma((pieces,)), dma((pieces,)),
        ]
        + weight_sems + weight_sems + spread_sems + spread_sems,
        compiler_params=pltpu.CompilerParams(
            collective_id=0, has_side_effects=True, vmem_limit_bytes=52 * 1024 * 1024
        ),
    )(
        tokens, bucket_ids.reshape(rows, 1), shift_table, scale_table, gate_table, w_qkv, w_out,
        q_gain.reshape(heads, HD), k_gain.reshape(heads, HD), cosine, sine, mask,
    )


def solution(mesh):
    in_specs = (
        P(("row", "depth"), "col"),
        P(("row", "depth")),
        P(),
        P(),
        P(),
        P(None, "col"),
        P("row", "col"),
        P("col"),
        P("col"),
        P("row", "col"),
    )
    out_specs = P(("row", "depth"), "col")
    return jax.shard_map(shards, mesh=mesh, in_specs=in_specs, out_specs=out_specs, check_vma=False)
```

```python
import functools
import math

import jax
import jax.numpy as jnp
from jax import lax
from jax.experimental import pallas as pl
from jax.experimental.pallas import tpu as pltpu
from jax.sharding import PartitionSpec as P

HD = 128
EPS = 1e-06
MESH = pl.DeviceIdType.MESH


def remote(src, dst, send, recv, device):
    return pltpu.make_async_remote_copy(
        src_ref=src, dst_ref=dst, send_sem=send, recv_sem=recv, device_id=device, device_id_type=MESH
    )


class Place:
    def __init__(self):
        row = lax.axis_index("row")
        depth = lax.axis_index("depth")
        self.zh = lax.axis_index("col")
        self.zl = row // 4
        self.x = row % 4
        self.y = depth // 2
        self.core = depth % 2
        self.z = self.zh * 2 + self.zl

    def at(self, x=None, y=None, z=None, core=None):
        x = self.x if x is None else x % 4
        y = self.y if y is None else y % 4
        z = self.z if z is None else z % 8
        core = self.core if core is None else core
        return ((z % 2) * 4 + x, z // 2, y * 2 + core)


class Weights:
    def __init__(self, at, tile, buf, sems, by_columns):
        self.at, self.tile, self.buf, self.by_columns = at, tile, buf, by_columns
        self.rows, self.cols = tile.shape
        (self.sx, self.rx, self.sf, self.rf, self.sy, self.ry, self.sc, self.rc, self.own) = sems

    def cut(self, ref, first, quarter, core):
        quarter_rows = self.rows // 4
        if self.by_columns:
            half = self.cols // 2
            return ref.at[
                pl.ds(pl.multiple_of(first + quarter * quarter_rows, 16), quarter_rows),
                pl.ds(pl.multiple_of(core * half, 128), half),
            ]
        half = quarter_rows // 2
        return ref.at[pl.ds(pl.multiple_of(first + quarter * quarter_rows + core * half, 16), half), :]

    def slot(self, x, quarter, core=None):
        core = self.at.core if core is None else core
        return self.cut(self.buf, (x % 4) * self.rows, quarter % 4, core)

    def x1(self, side, i):
        a = self.at
        to = a.x + 1 if side == 0 else a.x - 1
        return remote(
            self.cut(self.tile, 0, (a.y + i) % 4, a.core),
            self.slot(a.x, a.y + i),
            self.sx.at[side, i],
            self.rx.at[side, i],
            a.at(x=to),
        )

    def x2(self, side):
        a = self.at
        frm = a.x - 1 if side == 0 else a.x + 1
        to = a.x + 1 if side == 0 else a.x - 1
        ref = self.slot(frm, a.y + side)
        return remote(ref, ref, self.sf.at[side], self.rf.at[side], a.at(x=to))

    def y1(self, t, side):
        a = self.at
        ref = self.slot(a.x + t, a.y + side)
        to = a.y + 1 if side == 0 else a.y - 1
        return remote(ref, ref, self.sy.at[t - 1, side], self.ry.at[t - 1, side], a.at(y=to))

    def c1(self, t, i):
        a = self.at
        ref = self.slot(a.x + t, a.y + i)
        return remote(ref, ref, self.sc.at[t - 1, i], self.rc.at[t - 1, i], a.at(core=1 - a.core))

    def local(self):
        first = pl.multiple_of(self.at.x * self.rows, 16)
        return pltpu.make_async_copy(self.tile, self.buf.at[pl.ds(first, self.rows), :], self.own)

    def start(self):
        for side, i in ((0, 0), (1, 1), (0, 1), (1, 0)):
            self.x1(side, i).start()
        self.local().start()

    def near(self):
        for side in (0, 1):
            t = 3 if side == 0 else 1
            self.x1(side, side).wait_recv()
            self.x2(side).start()
            self.y1(t, side).start()
            self.c1(t, side).start()
        for side in (0, 1):
            t = 3 if side == 0 else 1
            self.x1(side, 1 - side).wait_recv()
            self.y1(t, 1 - side).start()
            self.c1(t, 1 - side).start()

    def far(self):
        for side in (0, 1):
            self.x2(side).wait_recv()
            self.y1(2, side).start()
            self.c1(2, side).start()

    def across(self):
        for t in (3, 1, 2):
            for side in (0, 1):
                self.y1(t, side).wait_recv()
                self.c1(t, 3 if side == 0 else 2).start()

    def ready(self):
        self.local().wait()
        for t in (3, 1, 2):
            for i in range(4):
                self.c1(t, i).wait_recv()

    def drain(self):
        for side in (0, 1):
            for i in (0, 1):
                self.x1(side, i).wait_send()
            self.x2(side).wait_send()
        for t in (1, 2, 3):
            for side in (0, 1):
                self.y1(t, side).wait_send()
            for i in range(4):
                self.c1(t, i).wait_send()


class Spread:
    SENDS = (
        ((2, 0), (6, 1), (2, 1), (6, 0)),
        ((1, 1), (7, 1), (3, 0), (5, 0), (1, 0), (7, 0)),
        ((2, 0), (6, 1), (2, 1), (6, 0)),
        ((1, 0), (1, 1), (5, 0), (5, 1), (7, 0), (7, 1)),
        ((7, 1), (3, 0), (3, 1), (5, 0), (1, 0), (1, 1), (7, 0)),
        ((2, 0), (6, 1), (2, 1), (6, 0)),
        ((1, 1), (5, 0), (5, 1), (3, 0), (1, 0), (7, 0), (7, 1)),
        ((2, 0), (2, 1), (6, 0), (6, 1)),
    )
    RELAYS = (
        ((1, 1, 6), (2, 1, 6)),
        ((3, 0, 2), (3, 1, 2)),
        ((0, 0, 2), (1, 1, 2)),
        ((0, 1, 6), (1, 1, 6)),
        ((3, 0, 2), (2, 0, 2), (3, 1, 2)),
        (),
        ((0, 1, 6),),
        ((1, 0, 2), (2, 1, 2)),
    )

    def __init__(self, at, src, buf, sems):
        self.at, self.src, self.buf = at, src, buf
        self.half, self.width = src.shape[0] // 2, src.shape[1]
        self.send, self.recv = sems

    def view(self, slot, half):
        column = slot // 2 * self.width
        return self.buf.at[slot % 2, pl.ds(half * self.half, self.half), pl.ds(column, self.width)]

    def own(self, half):
        return self.src.at[pl.ds(half * self.half, self.half), :]

    def out(self, z, i):
        go, half = self.SENDS[z][i]
        slot = z % 4
        return remote(
            self.own(half), self.view(slot, half), self.send.at[i], self.recv.at[slot, half], self.at.at(z=z + go)
        )

    def keep(self, z, half):
        slot = z % 4
        return pltpu.make_async_copy(self.own(half), self.view(slot, half), self.recv.at[slot, half])

    def came(self, slot, half):
        ref = self.view(slot, half)
        pltpu.make_async_copy(ref, ref, self.recv.at[slot, half]).wait()

    def forward(self, z, i):
        slot, half, go = self.RELAYS[z][i]
        ref = self.view(slot, half)
        return remote(
            ref, ref, self.send.at[len(self.SENDS[z]) + i], self.recv.at[slot, half], self.at.at(z=z + go)
        )

    def each(self, body):
        for z in range(8):
            pl.when(self.at.z == z)(functools.partial(body, z))

    def start(self):
        def body(z):
            for i in range(len(self.SENDS[z])):
                self.out(z, i).start()
            if z % 2 == z // 4:
                for half in (0, 1):
                    self.keep(z, half).start()

        self.each(body)

    def relay(self):
        def body(z):
            for i, (slot, half, _) in enumerate(self.RELAYS[z]):
                self.came(slot, half)
                self.forward(z, i).start()

        self.each(body)

    def ready(self):
        def body(z):
            taken = [(slot, half) for slot, half, _ in self.RELAYS[z]]
            for slot in range(4):
                for half in (0, 1):
                    if (slot, half) not in taken:
                        self.came(slot, half)

        self.each(body)

    def drain(self):
        def body(z):
            for i in range(len(self.SENDS[z])):
                self.out(z, i).wait_send()
            for i in range(len(self.RELAYS[z])):
                self.forward(z, i).wait_send()

        self.each(body)


def bucket_rows(pick, table):
    first = table.astype(jnp.bfloat16)
    rest = table - first.astype(jnp.float32)
    second = rest.astype(jnp.bfloat16)
    third = (rest - second.astype(jnp.float32)).astype(jnp.bfloat16)
    terms = jnp.concatenate([first, second, third], axis=0)
    return jnp.dot(pick, terms, preferred_element_type=jnp.float32)


def block_kernel(
    tokens_in, ids_in, clips_in, shift_in, scale_in, gate_in, wq, wo, qg_in, kg_in, out,
    tokens, ids, clips, shift, scale, gate, qg, kg, cosine, sine, mask, result, in_sem, out_sem,
    wq_all, wo_all, mod, a1, att, a2, row_a, row_b, stat_in, stat_col, stats,
    home1, mine1, theirs1, home2, mine2, theirs2, acc1, acc2,
    stat_send, stat_recv, c1_send, c1_recv, c2_send, c2_recv,
    qs0, qs1, qs2, qs3, qs4, qs5, qs6, qs7, qs8,
    os0, os1, os2, os3, os4, os5, os6, os7, os8,
    as0, as1, bs0, bs1,
):
    at = Place()
    wide = tokens.shape[1]
    heads = qg.shape[0] // HD
    buckets = shift.shape[0]
    here = pl.ds(pl.multiple_of(at.zh * wide, 128), wide)
    loads = [
        pltpu.make_async_copy(src, dst, in_sem.at[i])
        for i, (src, dst) in enumerate(
            [
                (tokens_in, tokens), (ids_in, ids), (scale_in.at[:, here], scale),
                (shift_in.at[:, here], shift), (gate_in, gate), (clips_in, clips),
                (qg_in, qg), (kg_in, kg),
            ]
        )
    ]
    for load in loads:
        load.start()

    barrier = pltpu.get_barrier_semaphore()
    friends = [at.at(z=at.z + o) for o in range(1, 8)]
    friends += [at.at(x=at.x + 1), at.at(x=at.x + 3), at.at(y=at.y + 1), at.at(y=at.y + 3)]
    friends += [at.at(core=1 - at.core)]
    for friend in friends:
        pl.semaphore_signal(barrier, inc=1, device_id=friend, device_id_type=MESH)
    pl.semaphore_wait(barrier, len(friends))

    qkv = Weights(at, wq, wq_all, (qs0, qs1, qs2, qs3, qs4, qs5, qs6, qs7, qs8), False)
    proj = Weights(at, wo, wo_all, (os0, os1, os2, os3, os4, os5, os6, os7, os8), True)
    one = Spread(at, mod, a1, (as0, as1))
    two = Spread(at, att, a2, (bs0, bs1))

    qkv.start()
    loads[0].wait()

    lane = lax.broadcasted_iota(jnp.int32, (16, HD), 1)

    @pl.loop(0, 8)
    def _(i):
        rows = pl.ds(pl.multiple_of(i * 16, 16), 16)
        part = tokens[rows, :].astype(jnp.float32)
        mean = jnp.sum(part, axis=1, keepdims=True) * (1.0 / wide)
        part = part - mean
        spread = jnp.sum(part * part, axis=1, keepdims=True)
        stat_in[rows, :] = jnp.where(lane == 0, mean, jnp.where(lane == 1, spread, 0.0))

    stats[at.zh] = stat_in[...].T[0:8, :]

    def stat_copy(o):
        ref = stats.at[at.zh]
        return remote(ref, ref, stat_send.at[o - 1], stat_recv.at[o - 1], at.at(z=at.z + 2 * o))

    for o in (1, 3, 2):
        stat_copy(o).start()

    for load in loads[1:]:
        load.wait()
    lanes = lax.broadcasted_iota(jnp.int32, (HD, HD), 1)
    index = lax.broadcasted_iota(jnp.int32, (HD, HD), 0)
    bucket = jnp.broadcast_to(ids[...].astype(jnp.float32), (HD, HD)).T.astype(jnp.int32)
    pick = (bucket[:, 0 : 3 * buckets] == lanes[:, 0 : 3 * buckets] % buckets).astype(jnp.bfloat16)
    row_a[...] = 1.0 + bucket_rows(pick, scale[...])
    row_b[...] = bucket_rows(pick, shift[...])

    for o in (1, 3, 2):
        stat_copy(o).wait_recv()
    means = [stats[c][0:1, :] for c in range(4)]
    mean = (means[0] + means[1] + means[2] + means[3]) * 0.25
    total = jnp.zeros_like(mean)
    for c in range(4):
        apart = means[c] - mean
        total = total + stats[c][1:2, :] + wide * (apart * apart)
    rstd = lax.rsqrt(total * (1.0 / (4 * wide)) + EPS)
    stat_col[...] = jnp.where(index == 0, mean, jnp.where(index == 1, rstd, 0.0)).T

    @pl.loop(0, 8)
    def _(i):
        rows = pl.ds(pl.multiple_of(i * 16, 16), 16)
        normed = (tokens[rows, :].astype(jnp.float32) - stat_col[rows, 0:1]) * stat_col[rows, 1:2]
        mod[rows, :] = (normed * row_a[rows, :] + row_b[rows, :]).astype(jnp.bfloat16)

    one.start()

    count = clips.shape[1]
    lengths = jnp.broadcast_to(clips[...], (8, count)).astype(jnp.bfloat16)
    before = (
        lax.broadcasted_iota(jnp.int32, (count, count), 0)
        <= lax.broadcasted_iota(jnp.int32, (count, count), 1)
    ).astype(jnp.bfloat16)
    ends = jnp.dot(lengths, before, preferred_element_type=jnp.float32)[0:1, :]
    first = (at.zl * 4 + at.x) * 8 + at.y * 2 + at.core
    token = (first * HD + lax.broadcasted_iota(jnp.int32, (HD, count), 0)).astype(jnp.float32)
    passed = ends <= token
    clip = jnp.sum(jnp.where(passed, 1.0, 0.0), axis=1, keepdims=True)
    begin = jnp.sum(
        jnp.where(passed, clips[...].astype(jnp.float32), 0.0), axis=1, keepdims=True
    )
    clip = jnp.broadcast_to(clip, (HD, HD))
    mask[...] = jnp.where(clip == clip.T, 1.0, 0.0)
    half = HD // 2
    power = (lanes[:, 0:half]).astype(jnp.float32) * (-math.log(10000.0) / half)
    angles = (token[:, 0:1] - begin) * jnp.exp(power)
    cosine_half, sine_half = jnp.cos(angles), jnp.sin(angles)
    cosine[...] = jnp.concatenate([cosine_half, cosine_half], axis=1)
    sine[...] = jnp.concatenate([-sine_half, sine_half], axis=1)

    qkv.near()
    proj.start()
    qkv.far()
    one.relay()
    qkv.across()
    proj.near()
    proj.far()
    row_a[...] = bucket_rows(pick, gate[...])
    qkv.ready()
    one.ready()

    pieces, piece = home2.shape[0], home2.shape[2]
    partner = at.at(z=at.zh * 2 + 1 - at.zl)
    own_rows = pl.ds(pl.multiple_of(at.zl * HD, HD), HD)
    other_rows = pl.ds(pl.multiple_of((1 - at.zl) * HD, HD), HD)

    def swap1(h):
        return remote(mine1.at[h], theirs1.at[h], c1_send.at[h], c1_recv.at[h], partner)

    def store(n):
        columns = pl.ds(pl.multiple_of(n * piece, HD), piece)
        return pltpu.make_async_copy(result.at[n], out.at[:, columns], out_sem.at[n])

    def swap2(h):
        return remote(mine2.at[h], theirs2.at[h], c2_send.at[h], c2_recv.at[h], partner)

    @pl.loop(0, heads)
    def _(h):
        columns = pl.ds(pl.multiple_of(h * (3 * HD), HD), 3 * HD)
        left = a1[...].reshape(2 * HD, a1.shape[2])
        acc1[...] = jnp.dot(left, wq_all[:, columns], preferred_element_type=jnp.float32)
        mine1[h] = acc1[other_rows, :].astype(jnp.bfloat16)
        swap1(h).start()
        home1[h] = acc1[own_rows, :]

    proj.across()

    def rotate(vectors, gains):
        power = jnp.mean(vectors * vectors, axis=-1, keepdims=True)
        vectors = vectors * lax.rsqrt(power + EPS) * gains
        turned = pltpu.roll(vectors, HD // 2, axis=1)
        return (vectors * cosine[...] + turned * sine[...]).astype(jnp.bfloat16)

    @pl.loop(0, heads)
    def _(h):
        swap1(h).wait_recv()
        head = pl.ds(pl.multiple_of(h * HD, HD), HD)
        joined = home1[h] + theirs1[h].astype(jnp.float32)
        query = rotate(joined[:, 0:HD], qg[head].reshape(1, HD))
        key = rotate(joined[:, HD : 2 * HD], kg[head].reshape(1, HD))
        value = joined[:, 2 * HD : 3 * HD].astype(jnp.bfloat16)
        scores = lax.dot_general(
            query, key, (((1,), (1,)), ((), ())), preferred_element_type=jnp.float32
        ) * (1.0 / math.sqrt(HD))
        raised = jnp.where(mask[...] > 0.0, jnp.exp(scores), 0.0)
        weights = (raised / jnp.sum(raised, axis=-1, keepdims=True)).astype(jnp.bfloat16)
        att[:, head] = jnp.dot(weights, value, preferred_element_type=jnp.float32).astype(
            jnp.bfloat16
        )

    two.start()
    proj.ready()
    two.relay()
    two.ready()

    @pl.loop(0, pieces)
    def _(n):
        columns = pl.ds(pl.multiple_of(n * piece, HD), piece)
        left = a2[...].reshape(2 * HD, a2.shape[2])
        acc2[...] = jnp.dot(left, wo_all[:, columns], preferred_element_type=jnp.float32)
        mine2[n] = acc2[other_rows, :].astype(jnp.bfloat16)
        swap2(n).start()
        home2[n] = acc2[own_rows, :]

    qkv.drain()
    proj.drain()
    one.drain()
    two.drain()
    for o in (1, 2, 3):
        stat_copy(o).wait_send()

    @pl.loop(0, heads)
    def _(h):
        swap1(h).wait_send()

    @pl.loop(0, pieces)
    def _(n):
        columns = pl.ds(pl.multiple_of(n * piece, HD), piece)
        swap2(n).wait_recv()
        projected = home2[n] + theirs2[n].astype(jnp.float32)
        result[n] = (row_a[:, columns] * projected).astype(jnp.bfloat16)
        store(n).start()

    @pl.loop(0, pieces)
    def _(n):
        swap2(n).wait_send()
        store(n).wait()


def shards(
    tokens, bucket_ids, clip_lengths, shift_table, scale_table, gate_table, w_qkv, q_gain, k_gain, w_out
):
    rows, wide = tokens.shape
    heads = w_qkv.shape[1] // (3 * HD)
    pieces = 5
    piece = wide // pieces
    bf16, f32 = jnp.bfloat16, jnp.float32
    dma = pltpu.SemaphoreType.DMA
    weight_sems = [dma((2, 2)), dma((2, 2)), dma((2,)), dma((2,)), dma((3, 2)), dma((3, 2)), dma((3, 4)), dma((3, 4)), dma]
    spread_sems = [dma((10,)), dma((4, 2))]
    hbm = pl.BlockSpec(memory_space=pltpu.HBM)
    return pl.pallas_call(
        block_kernel,
        out_shape=jax.ShapeDtypeStruct((rows, wide), bf16),
        in_specs=[hbm] * 10,
        out_specs=hbm,
        scratch_shapes=[
            pltpu.VMEM((rows, wide), bf16),
            pltpu.VMEM((1, rows), jnp.int32),
            pltpu.VMEM((1, clip_lengths.shape[0]), jnp.int32),
            pltpu.VMEM((shift_table.shape[0], wide), f32),
            pltpu.VMEM((shift_table.shape[0], wide), f32),
            pltpu.VMEM((shift_table.shape[0], wide), f32),
            pltpu.VMEM((heads * HD,), f32),
            pltpu.VMEM((heads * HD,), f32),
            pltpu.VMEM((rows, HD), f32),
            pltpu.VMEM((rows, HD), f32),
            pltpu.VMEM((rows, rows), f32),
            pltpu.VMEM((pieces, rows, piece), bf16),
            dma((8,)),
            dma((pieces,)),
            pltpu.VMEM((4 * w_qkv.shape[0], w_qkv.shape[1]), bf16),
            pltpu.VMEM((4 * w_out.shape[0], w_out.shape[1]), bf16),
            pltpu.VMEM((rows, wide), bf16),
            pltpu.VMEM((2, rows, 2 * wide), bf16),
            pltpu.VMEM((rows, heads * HD), bf16),
            pltpu.VMEM((2, rows, 2 * heads * HD), bf16),
            pltpu.VMEM((rows, wide), f32),
            pltpu.VMEM((rows, wide), f32),
            pltpu.VMEM((rows, HD), f32),
            pltpu.VMEM((rows, HD), f32),
            pltpu.VMEM((4, 8, rows), f32),
            pltpu.VMEM((heads, rows, 3 * HD), f32),
            pltpu.VMEM((heads, rows, 3 * HD), bf16),
            pltpu.VMEM((heads, rows, 3 * HD), bf16),
            pltpu.VMEM((pieces, rows, piece), f32),
            pltpu.VMEM((pieces, rows, piece), bf16),
            pltpu.VMEM((pieces, rows, piece), bf16),
            pltpu.VMEM((2 * rows, 3 * HD), f32),
            pltpu.VMEM((2 * rows, piece), f32),
            dma((3,)), dma((3,)),
            dma((heads,)), dma((heads,)),
            dma((pieces,)), dma((pieces,)),
        ]
        + weight_sems + weight_sems + spread_sems + spread_sems,
        compiler_params=pltpu.CompilerParams(
            collective_id=0, has_side_effects=True, vmem_limit_bytes=60 * 1024 * 1024
        ),
    )(
        tokens, bucket_ids.reshape(1, rows), clip_lengths.reshape(1, -1), shift_table, scale_table, gate_table,
        w_qkv, w_out, q_gain, k_gain,
    )


def solution(mesh):
    in_specs = (
        P(("row", "depth"), "col"),
        P(("row", "depth")),
        P(),
        P(),
        P(),
        P(None, "col"),
        P("row", "col"),
        P("col"),
        P("col"),
        P("row", "col"),
    )
    out_specs = P(("row", "depth"), "col")
    return jax.shard_map(shards, mesh=mesh, in_specs=in_specs, out_specs=out_specs, check_vma=False)
```

```python
import functools
import math

import jax
import jax.numpy as jnp
from jax import lax
from jax.experimental import pallas as pl
from jax.experimental.pallas import tpu as pltpu
from jax.sharding import PartitionSpec as P

HD = 128
EPS = 1e-06
MESH = pl.DeviceIdType.MESH


def remote(src, dst, send, recv, device):
    return pltpu.make_async_remote_copy(
        src_ref=src, dst_ref=dst, send_sem=send, recv_sem=recv, device_id=device, device_id_type=MESH
    )


class Place:
    def __init__(self):
        row = lax.axis_index("row")
        depth = lax.axis_index("depth")
        self.zh = lax.axis_index("col")
        self.zl = row // 4
        self.x = row % 4
        self.y = depth // 2
        self.core = depth % 2
        self.z = self.zh * 2 + self.zl

    def at(self, x=None, y=None, z=None, core=None):
        x = self.x if x is None else x % 4
        y = self.y if y is None else y % 4
        z = self.z if z is None else z % 8
        core = self.core if core is None else core
        return ((z % 2) * 4 + x, z // 2, y * 2 + core)


class Weights:
    def __init__(self, at, tile, buf, sems, by_columns):
        self.at, self.tile, self.buf, self.by_columns = at, tile, buf, by_columns
        self.rows, self.cols = tile.shape
        (self.sx, self.rx, self.sf, self.rf, self.sy, self.ry, self.sc, self.rc, self.own) = sems

    def cut(self, ref, first, quarter, core):
        quarter_rows = self.rows // 4
        if self.by_columns:
            half = self.cols // 2
            return ref.at[
                pl.ds(pl.multiple_of(first + quarter * quarter_rows, 16), quarter_rows),
                pl.ds(pl.multiple_of(core * half, 128), half),
            ]
        half = quarter_rows // 2
        return ref.at[pl.ds(pl.multiple_of(first + quarter * quarter_rows + core * half, 16), half), :]

    def slot(self, x, quarter, core=None):
        core = self.at.core if core is None else core
        return self.cut(self.buf, (x % 4) * self.rows, quarter % 4, core)

    def x1(self, side, i):
        a = self.at
        to = a.x + 1 if side == 0 else a.x - 1
        return remote(
            self.cut(self.tile, 0, (a.y + i) % 4, a.core),
            self.slot(a.x, a.y + i),
            self.sx.at[side, i],
            self.rx.at[side, i],
            a.at(x=to),
        )

    def x2(self, side):
        a = self.at
        frm = a.x - 1 if side == 0 else a.x + 1
        to = a.x + 1 if side == 0 else a.x - 1
        ref = self.slot(frm, a.y + side)
        return remote(ref, ref, self.sf.at[side], self.rf.at[side], a.at(x=to))

    def y1(self, t, side):
        a = self.at
        ref = self.slot(a.x + t, a.y + side)
        to = a.y + 1 if side == 0 else a.y - 1
        return remote(ref, ref, self.sy.at[t - 1, side], self.ry.at[t - 1, side], a.at(y=to))

    def c1(self, t, i):
        a = self.at
        ref = self.slot(a.x + t, a.y + i)
        return remote(ref, ref, self.sc.at[t - 1, i], self.rc.at[t - 1, i], a.at(core=1 - a.core))

    def local(self):
        first = pl.multiple_of(self.at.x * self.rows, 16)
        return pltpu.make_async_copy(self.tile, self.buf.at[pl.ds(first, self.rows), :], self.own)

    def start(self):
        for side, i in ((0, 0), (1, 1), (0, 1), (1, 0)):
            self.x1(side, i).start()
        self.local().start()

    def near(self):
        for side in (0, 1):
            t = 3 if side == 0 else 1
            self.x1(side, side).wait_recv()
            self.x2(side).start()
            self.y1(t, side).start()
            self.c1(t, side).start()
        for side in (0, 1):
            t = 3 if side == 0 else 1
            self.x1(side, 1 - side).wait_recv()
            self.y1(t, 1 - side).start()
            self.c1(t, 1 - side).start()

    def far(self):
        for side in (0, 1):
            self.x2(side).wait_recv()
            self.y1(2, side).start()
            self.c1(2, side).start()

    def across(self):
        for t in (3, 1, 2):
            for side in (0, 1):
                self.y1(t, side).wait_recv()
                self.c1(t, 3 if side == 0 else 2).start()

    def ready(self):
        self.local().wait()
        for t in (3, 1, 2):
            for i in range(4):
                self.c1(t, i).wait_recv()

    def drain(self):
        for side in (0, 1):
            for i in (0, 1):
                self.x1(side, i).wait_send()
            self.x2(side).wait_send()
        for t in (1, 2, 3):
            for side in (0, 1):
                self.y1(t, side).wait_send()
            for i in range(4):
                self.c1(t, i).wait_send()


class Spread:
    SENDS = (
        ((2, 0), (6, 1), (2, 1), (6, 0)),
        ((1, 1), (7, 1), (3, 0), (5, 0), (1, 0), (7, 0)),
        ((2, 0), (6, 1), (2, 1), (6, 0)),
        ((1, 0), (1, 1), (5, 0), (5, 1), (7, 0), (7, 1)),
        ((7, 1), (3, 0), (3, 1), (5, 0), (1, 0), (1, 1), (7, 0)),
        ((2, 0), (6, 1), (2, 1), (6, 0)),
        ((1, 1), (5, 0), (5, 1), (3, 0), (1, 0), (7, 0), (7, 1)),
        ((2, 0), (2, 1), (6, 0), (6, 1)),
    )
    RELAYS = (
        ((1, 1, 6), (2, 1, 6)),
        ((3, 0, 2), (3, 1, 2)),
        ((0, 0, 2), (1, 1, 2)),
        ((0, 1, 6), (1, 1, 6)),
        ((3, 0, 2), (2, 0, 2), (3, 1, 2)),
        (),
        ((0, 1, 6),),
        ((1, 0, 2), (2, 1, 2)),
    )

    def __init__(self, at, src, buf, sems):
        self.at, self.src, self.buf = at, src, buf
        self.half, self.width = src.shape[0] // 2, src.shape[1]
        self.send, self.recv = sems

    def view(self, slot, half):
        column = slot // 2 * self.width
        return self.buf.at[slot % 2, pl.ds(half * self.half, self.half), pl.ds(column, self.width)]

    def own(self, half):
        return self.src.at[pl.ds(half * self.half, self.half), :]

    def out(self, z, i):
        go, half = self.SENDS[z][i]
        slot = z % 4
        return remote(
            self.own(half), self.view(slot, half), self.send.at[i], self.recv.at[slot, half], self.at.at(z=z + go)
        )

    def keep(self, z, half):
        slot = z % 4
        return pltpu.make_async_copy(self.own(half), self.view(slot, half), self.recv.at[slot, half])

    def came(self, slot, half):
        ref = self.view(slot, half)
        pltpu.make_async_copy(ref, ref, self.recv.at[slot, half]).wait()

    def forward(self, z, i):
        slot, half, go = self.RELAYS[z][i]
        ref = self.view(slot, half)
        return remote(
            ref, ref, self.send.at[len(self.SENDS[z]) + i], self.recv.at[slot, half], self.at.at(z=z + go)
        )

    def each(self, body):
        for z in range(8):
            pl.when(self.at.z == z)(functools.partial(body, z))

    def start(self):
        def body(z):
            for i in range(len(self.SENDS[z])):
                self.out(z, i).start()
            if z % 2 == z // 4:
                for half in (0, 1):
                    self.keep(z, half).start()

        self.each(body)

    def relay(self, turns=(0, 1, 2)):
        def body(z):
            for i, (slot, half, _) in enumerate(self.RELAYS[z]):
                if i in turns:
                    self.came(slot, half)
                    self.forward(z, i).start()

        self.each(body)

    def ready(self, slots=(0, 1, 2, 3)):
        def body(z):
            taken = [(slot, half) for slot, half, _ in self.RELAYS[z]]
            for slot in slots:
                for half in (0, 1):
                    if (slot, half) not in taken:
                        self.came(slot, half)

        self.each(body)

    def drain(self):
        def body(z):
            for i in range(len(self.SENDS[z])):
                self.out(z, i).wait_send()
            for i in range(len(self.RELAYS[z])):
                self.forward(z, i).wait_send()

        self.each(body)


def bucket_rows(pick, table):
    first = table.astype(jnp.bfloat16)
    rest = table - first.astype(jnp.float32)
    second = rest.astype(jnp.bfloat16)
    third = (rest - second.astype(jnp.float32)).astype(jnp.bfloat16)
    terms = jnp.concatenate([first, second, third], axis=0)
    return jnp.dot(pick, terms, preferred_element_type=jnp.float32)


def block_kernel(
    tokens_in, ids_in, clips_in, shift_in, scale_in, gate_in, wq, wo, qg_in, kg_in, out,
    tokens, ids, their_ids, clips, shift, scale, gate, qg, kg, cosine, sine, mask, result, in_sem, out_sem, id_sem,
    wq_all, wo_all, raw, a1, att, a2, row_a, row_b, row_gate, stat_in, stat_col, stats,
    home1, mine1, theirs1, home2, mine2, theirs2, acc1, acc2,
    stat_send, stat_recv, c1_send, c1_recv, c2_send, c2_recv,
    qs0, qs1, qs2, qs3, qs4, qs5, qs6, qs7, qs8,
    os0, os1, os2, os3, os4, os5, os6, os7, os8,
    as0, as1, bs0, bs1,
):
    at = Place()
    wide = tokens.shape[1]
    heads = qg.shape[0] // HD
    buckets = shift.shape[0]
    here = pl.ds(pl.multiple_of(at.zl * (2 * wide), 128), 2 * wide)
    loads = [
        pltpu.make_async_copy(src, dst, in_sem.at[i])
        for i, (src, dst) in enumerate(
            [
                (tokens_in, tokens), (ids_in, ids), (scale_in.at[:, here], scale),
                (shift_in.at[:, here], shift), (gate_in, gate), (clips_in, clips),
                (qg_in, qg), (kg_in, kg),
            ]
        )
    ]
    for load in loads:
        load.start()

    barrier = pltpu.get_barrier_semaphore()
    friends = [at.at(z=at.z + o) for o in range(1, 8)]
    friends += [at.at(x=at.x + 1), at.at(x=at.x + 3), at.at(y=at.y + 1), at.at(y=at.y + 3)]
    friends += [at.at(core=1 - at.core)]
    for friend in friends:
        pl.semaphore_signal(barrier, inc=1, device_id=friend, device_id_type=MESH)
    pl.semaphore_wait(barrier, len(friends))

    qkv = Weights(at, wq, wq_all, (qs0, qs1, qs2, qs3, qs4, qs5, qs6, qs7, qs8), False)
    proj = Weights(at, wo, wo_all, (os0, os1, os2, os3, os4, os5, os6, os7, os8), True)
    one = Spread(at, tokens_in, raw, (as0, as1))
    two = Spread(at, att, a2, (bs0, bs1))

    partner = at.at(z=at.zh * 2 + 1 - at.zl)
    loads[1].wait()
    id_copy = remote(ids, their_ids, id_sem.at[0], id_sem.at[1], partner)
    id_copy.start()
    one.start()
    qkv.start()
    for i, load in enumerate(loads):
        if i != 1:
            load.wait()

    lane = lax.broadcasted_iota(jnp.int32, (16, HD), 1)

    @pl.loop(0, 8)
    def _(i):
        rows = pl.ds(pl.multiple_of(i * 16, 16), 16)
        part = tokens[rows, :].astype(jnp.float32)
        mean = jnp.sum(part, axis=1, keepdims=True) * (1.0 / wide)
        part = part - mean
        spread = jnp.sum(part * part, axis=1, keepdims=True)
        stat_in[rows, :] = jnp.where(lane == 0, mean, jnp.where(lane == 1, spread, 0.0))

    index = lax.broadcasted_iota(jnp.int32, (HD, HD), 0)
    lanes = lax.broadcasted_iota(jnp.int32, (HD, HD), 1)
    stats[at.z] = stat_in[...].T[0:8, :]

    def stat_copy(o):
        ref = stats.at[at.z]
        return remote(ref, ref, stat_send.at[o - 1], stat_recv.at[o - 1], at.at(z=at.z + o))

    for o in range(1, 8):
        stat_copy(o).start()

    qkv.near()
    one.relay()
    count = clips.shape[1]
    lengths = jnp.broadcast_to(clips[...], (8, count)).astype(jnp.bfloat16)
    before = (
        lax.broadcasted_iota(jnp.int32, (count, count), 0)
        <= lax.broadcasted_iota(jnp.int32, (count, count), 1)
    ).astype(jnp.bfloat16)
    ends = jnp.dot(lengths, before, preferred_element_type=jnp.float32)[0:1, :]
    first = (at.zl * 4 + at.x) * 8 + at.y * 2 + at.core
    token = (first * HD + lax.broadcasted_iota(jnp.int32, (HD, count), 0)).astype(jnp.float32)
    passed = ends <= token
    clip = jnp.sum(jnp.where(passed, 1.0, 0.0), axis=1, keepdims=True)
    begin = jnp.sum(jnp.where(passed, clips[...].astype(jnp.float32), 0.0), axis=1, keepdims=True)
    clip = jnp.broadcast_to(clip, (HD, HD))
    mask[...] = jnp.where(clip == clip.T, 1.0, 0.0)
    half = HD // 2
    power = (lanes[:, 0:half]).astype(jnp.float32) * (-math.log(10000.0) / half)
    angles = (token[:, 0:1] - begin) * jnp.exp(power)
    cosine_half, sine_half = jnp.cos(angles), jnp.sin(angles)
    cosine[...] = jnp.concatenate([cosine_half, cosine_half], axis=1)
    sine[...] = jnp.concatenate([-sine_half, sine_half], axis=1)

    def bucket_rows_of(bucket, table):
        bucket = jnp.broadcast_to(bucket[...].astype(jnp.float32), (HD, HD)).T.astype(jnp.int32)
        pick = (bucket[:, 0 : 3 * buckets] == lanes[:, 0 : 3 * buckets] % buckets).astype(jnp.bfloat16)
        return bucket_rows(pick, table[...])

    row_a[at.zl] = 1.0 + bucket_rows_of(ids, scale)
    row_b[at.zl] = bucket_rows_of(ids, shift)
    row_gate[...] = bucket_rows_of(ids, gate)
    id_copy.wait()
    row_a[1 - at.zl] = 1.0 + bucket_rows_of(their_ids, scale)
    row_b[1 - at.zl] = bucket_rows_of(their_ids, shift)

    qkv.far()
    proj.start()
    qkv.across()

    for o in range(1, 8):
        stat_copy(o).wait_recv()

    for block in (0, 1):
        parts = [stats[2 * c + block] for c in range(4)]
        mean = (parts[0][0:1] + parts[1][0:1] + parts[2][0:1] + parts[3][0:1]) * 0.25
        total = jnp.zeros_like(mean)
        for part in parts:
            apart = part[0:1] - mean
            total = total + part[1:2] + wide * (apart * apart)
        rstd = lax.rsqrt(total * (1.0 / (4 * wide)) + EPS)
        stat_col[block] = jnp.where(index == 0, mean, jnp.where(index == 1, rstd, 0.0)).T

    for slot in range(4):
        one.ready((slot,))
        block, part = slot % 2, pl.ds(slot // 2 * wide, wide)

        @pl.loop(0, 8)
        def _(i):
            rows = pl.ds(pl.multiple_of(i * 16, 16), 16)
            normed = raw[block, rows, part].astype(jnp.float32) - stat_col[block, rows, 0:1]
            normed = normed * stat_col[block, rows, 1:2]
            a1[block, rows, part] = (normed * row_a[block, rows, part] + row_b[block, rows, part]).astype(
                jnp.bfloat16
            )

    qkv.ready()

    pieces, piece = home2.shape[0], home2.shape[2]
    own_rows = pl.ds(pl.multiple_of(at.zl * HD, HD), HD)
    other_rows = pl.ds(pl.multiple_of((1 - at.zl) * HD, HD), HD)

    def swap1(h):
        return remote(mine1.at[h], theirs1.at[h], c1_send.at[h], c1_recv.at[h], partner)

    def store(n):
        columns = pl.ds(pl.multiple_of(n * piece, HD), piece)
        return pltpu.make_async_copy(result.at[n], out.at[:, columns], out_sem.at[n])

    def swap2(h):
        return remote(mine2.at[h], theirs2.at[h], c2_send.at[h], c2_recv.at[h], partner)

    @pl.loop(0, heads)
    def _(h):
        columns = pl.ds(pl.multiple_of(h * (3 * HD), HD), 3 * HD)
        left = a1[...].reshape(2 * HD, a1.shape[2])
        acc1[...] = jnp.dot(left, wq_all[:, columns], preferred_element_type=jnp.float32)
        mine1[h] = acc1[other_rows, :].astype(jnp.bfloat16)
        swap1(h).start()
        home1[h] = acc1[own_rows, :]

    proj.near()

    def rotate(vectors, gains):
        power = jnp.mean(vectors * vectors, axis=-1, keepdims=True)
        vectors = vectors * lax.rsqrt(power + EPS) * gains
        turned = pltpu.roll(vectors, HD // 2, axis=1)
        return (vectors * cosine[...] + turned * sine[...]).astype(jnp.bfloat16)

    @pl.loop(0, heads)
    def _(h):
        swap1(h).wait_recv()
        head = pl.ds(pl.multiple_of(h * HD, HD), HD)
        joined = home1[h] + theirs1[h].astype(jnp.float32)
        query = rotate(joined[:, 0:HD], qg[head].reshape(1, HD))
        key = rotate(joined[:, HD : 2 * HD], kg[head].reshape(1, HD))
        value = joined[:, 2 * HD : 3 * HD].astype(jnp.bfloat16)
        scores = lax.dot_general(
            query, key, (((1,), (1,)), ((), ())), preferred_element_type=jnp.float32
        ) * (1.0 / math.sqrt(HD))
        raised = jnp.where(mask[...] > 0.0, jnp.exp(scores), 0.0)
        weights = (raised / jnp.sum(raised, axis=-1, keepdims=True)).astype(jnp.bfloat16)
        att[:, head] = jnp.dot(weights, value, preferred_element_type=jnp.float32).astype(
            jnp.bfloat16
        )

    two.start()
    proj.far()
    two.relay()
    proj.across()
    proj.ready()
    two.ready()

    @pl.loop(0, pieces)
    def _(n):
        columns = pl.ds(pl.multiple_of(n * piece, HD), piece)
        left = a2[...].reshape(2 * HD, a2.shape[2])
        acc2[...] = jnp.dot(left, wo_all[:, columns], preferred_element_type=jnp.float32)
        mine2[n] = acc2[other_rows, :].astype(jnp.bfloat16)
        swap2(n).start()
        home2[n] = acc2[own_rows, :]

    qkv.drain()
    proj.drain()
    one.drain()
    two.drain()
    for o in range(1, 8):
        stat_copy(o).wait_send()

    @pl.loop(0, heads)
    def _(h):
        swap1(h).wait_send()

    @pl.loop(0, pieces)
    def _(n):
        columns = pl.ds(pl.multiple_of(n * piece, HD), piece)
        swap2(n).wait_recv()
        projected = home2[n] + theirs2[n].astype(jnp.float32)
        result[n] = (row_gate[:, columns] * projected).astype(jnp.bfloat16)
        store(n).start()

    @pl.loop(0, pieces)
    def _(n):
        swap2(n).wait_send()
        store(n).wait()


def shards(
    tokens, bucket_ids, clip_lengths, shift_table, scale_table, gate_table, w_qkv, q_gain, k_gain, w_out
):
    rows, wide = tokens.shape
    heads = w_qkv.shape[1] // (3 * HD)
    pieces = 5
    piece = wide // pieces
    bf16, f32 = jnp.bfloat16, jnp.float32
    dma = pltpu.SemaphoreType.DMA
    weight_sems = [dma((2, 2)), dma((2, 2)), dma((2,)), dma((2,)), dma((3, 2)), dma((3, 2)), dma((3, 4)), dma((3, 4)), dma]
    spread_sems = [dma((10,)), dma((4, 2))]
    hbm = pl.BlockSpec(memory_space=pltpu.HBM)
    return pl.pallas_call(
        block_kernel,
        out_shape=jax.ShapeDtypeStruct((rows, wide), bf16),
        in_specs=[hbm] * 10,
        out_specs=hbm,
        scratch_shapes=[
            pltpu.VMEM((rows, wide), bf16),
            pltpu.VMEM((1, rows), jnp.int32),
            pltpu.VMEM((1, rows), jnp.int32),
            pltpu.VMEM((1, clip_lengths.shape[0]), jnp.int32),
            pltpu.VMEM((shift_table.shape[0], 2 * wide), f32),
            pltpu.VMEM((shift_table.shape[0], 2 * wide), f32),
            pltpu.VMEM((shift_table.shape[0], wide), f32),
            pltpu.VMEM((heads * HD,), f32),
            pltpu.VMEM((heads * HD,), f32),
            pltpu.VMEM((rows, HD), f32),
            pltpu.VMEM((rows, HD), f32),
            pltpu.VMEM((rows, rows), f32),
            pltpu.VMEM((pieces, rows, piece), bf16),
            dma((8,)),
            dma((pieces,)),
            dma((2,)),
            pltpu.VMEM((4 * w_qkv.shape[0], w_qkv.shape[1]), bf16),
            pltpu.VMEM((4 * w_out.shape[0], w_out.shape[1]), bf16),
            pltpu.VMEM((2, rows, 2 * wide), bf16),
            pltpu.VMEM((2, rows, 2 * wide), bf16),
            pltpu.VMEM((rows, heads * HD), bf16),
            pltpu.VMEM((2, rows, 2 * heads * HD), bf16),
            pltpu.VMEM((2, rows, 2 * wide), f32),
            pltpu.VMEM((2, rows, 2 * wide), f32),
            pltpu.VMEM((rows, wide), f32),
            pltpu.VMEM((rows, HD), f32),
            pltpu.VMEM((2, rows, HD), f32),
            pltpu.VMEM((8, 8, rows), f32),
            pltpu.VMEM((heads, rows, 3 * HD), f32),
            pltpu.VMEM((heads, rows, 3 * HD), bf16),
            pltpu.VMEM((heads, rows, 3 * HD), bf16),
            pltpu.VMEM((pieces, rows, piece), f32),
            pltpu.VMEM((pieces, rows, piece), bf16),
            pltpu.VMEM((pieces, rows, piece), bf16),
            pltpu.VMEM((2 * rows, 3 * HD), f32),
            pltpu.VMEM((2 * rows, piece), f32),
            dma((7,)), dma((7,)),
            dma((heads,)), dma((heads,)),
            dma((pieces,)), dma((pieces,)),
        ]
        + weight_sems + weight_sems + spread_sems + spread_sems,
        compiler_params=pltpu.CompilerParams(
            collective_id=0, has_side_effects=True, vmem_limit_bytes=60 * 1024 * 1024
        ),
    )(
        tokens, bucket_ids.reshape(1, rows), clip_lengths.reshape(1, -1), shift_table, scale_table, gate_table,
        w_qkv, w_out, q_gain, k_gain,
    )


def solution(mesh):
    in_specs = (
        P(("row", "depth"), "col"),
        P(("row", "depth")),
        P(),
        P(),
        P(),
        P(None, "col"),
        P("row", "col"),
        P("col"),
        P("col"),
        P("row", "col"),
    )
    out_specs = P(("row", "depth"), "col")
    return jax.shard_map(shards, mesh=mesh, in_specs=in_specs, out_specs=out_specs, check_vma=False)
```

```python
import functools
import math

import jax
import jax.numpy as jnp
from jax import lax
from jax.experimental import pallas as pl
from jax.experimental.pallas import tpu as pltpu
from jax.sharding import PartitionSpec as P

HD = 128
EPS = 1e-06
MESH = pl.DeviceIdType.MESH


def remote(src, dst, send, recv, device):
    return pltpu.make_async_remote_copy(
        src_ref=src, dst_ref=dst, send_sem=send, recv_sem=recv, device_id=device, device_id_type=MESH
    )


class Place:
    def __init__(self):
        row = lax.axis_index("row")
        depth = lax.axis_index("depth")
        self.zh = lax.axis_index("col")
        self.zl = row // 4
        self.x = row % 4
        self.y = depth // 2
        self.core = depth % 2
        self.z = self.zh * 2 + self.zl

    def at(self, x=None, y=None, z=None, core=None):
        x = self.x if x is None else x % 4
        y = self.y if y is None else y % 4
        z = self.z if z is None else z % 8
        core = self.core if core is None else core
        return ((z % 2) * 4 + x, z // 2, y * 2 + core)


class Weights:
    def __init__(self, at, tile, buf, sems, by_columns, base=0):
        self.at, self.tile, self.buf, self.by_columns, self.base = at, tile, buf, by_columns, base
        self.rows, self.cols = tile.shape
        (self.sx, self.rx, self.sf, self.rf, self.sy, self.ry, self.sc, self.rc, self.own) = sems

    def cut(self, ref, first, quarter, core):
        quarter_rows = self.rows // 4
        if self.by_columns:
            half = self.cols // 2
            return ref.at[
                pl.ds(pl.multiple_of(first + quarter * quarter_rows, 16), quarter_rows),
                pl.ds(pl.multiple_of(core * half, 128), half),
            ]
        half = quarter_rows // 2
        return ref.at[pl.ds(pl.multiple_of(first + quarter * quarter_rows + core * half, 16), half), :]

    def slot(self, x, quarter, core=None):
        core = self.at.core if core is None else core
        return self.cut(self.buf, self.base + (x % 4) * self.rows, quarter % 4, core)

    def x1(self, side, i):
        a = self.at
        to = a.x + 1 if side == 0 else a.x - 1
        return remote(
            self.cut(self.tile, 0, (a.y + i) % 4, a.core),
            self.slot(a.x, a.y + i),
            self.sx.at[side, i],
            self.rx.at[side, i],
            a.at(x=to),
        )

    def x2(self, side):
        a = self.at
        frm = a.x - 1 if side == 0 else a.x + 1
        to = a.x + 1 if side == 0 else a.x - 1
        ref = self.slot(frm, a.y + side)
        return remote(ref, ref, self.sf.at[side], self.rf.at[side], a.at(x=to))

    def y1(self, t, side):
        a = self.at
        ref = self.slot(a.x + t, a.y + side)
        to = a.y + 1 if side == 0 else a.y - 1
        return remote(ref, ref, self.sy.at[t - 1, side], self.ry.at[t - 1, side], a.at(y=to))

    def c1(self, t, i):
        a = self.at
        ref = self.slot(a.x + t, a.y + i)
        return remote(ref, ref, self.sc.at[t - 1, i], self.rc.at[t - 1, i], a.at(core=1 - a.core))

    def local(self):
        first = pl.multiple_of(self.base + self.at.x * self.rows, 16)
        return pltpu.make_async_copy(self.tile, self.buf.at[pl.ds(first, self.rows), :], self.own)

    def start(self):
        for side, i in ((0, 0), (1, 1), (0, 1), (1, 0)):
            self.x1(side, i).start()
        self.local().start()

    def near(self):
        for side in (0, 1):
            t = 3 if side == 0 else 1
            self.x1(side, side).wait_recv()
            self.x2(side).start()
            self.y1(t, side).start()
            self.c1(t, side).start()
        for side in (0, 1):
            t = 3 if side == 0 else 1
            self.x1(side, 1 - side).wait_recv()
            self.y1(t, 1 - side).start()
            self.c1(t, 1 - side).start()

    def far(self):
        for side in (0, 1):
            self.x2(side).wait_recv()
            self.y1(2, side).start()
            self.c1(2, side).start()

    def across(self):
        for t in (3, 1, 2):
            for side in (0, 1):
                self.y1(t, side).wait_recv()
                self.c1(t, 3 if side == 0 else 2).start()

    def ready(self):
        self.local().wait()
        for t in (3, 1, 2):
            for i in range(4):
                self.c1(t, i).wait_recv()

    def drain(self):
        for side in (0, 1):
            for i in (0, 1):
                self.x1(side, i).wait_send()
            self.x2(side).wait_send()
        for t in (1, 2, 3):
            for side in (0, 1):
                self.y1(t, side).wait_send()
            for i in range(4):
                self.c1(t, i).wait_send()


class Spread:
    SENDS = (
        ((2, 0), (6, 1), (2, 1), (6, 0)),
        ((1, 1), (7, 1), (3, 0), (5, 0), (1, 0), (7, 0)),
        ((2, 0), (6, 1), (2, 1), (6, 0)),
        ((1, 0), (1, 1), (5, 0), (5, 1), (7, 0), (7, 1)),
        ((7, 1), (3, 0), (3, 1), (5, 0), (1, 0), (1, 1), (7, 0)),
        ((2, 0), (6, 1), (2, 1), (6, 0)),
        ((1, 1), (5, 0), (5, 1), (3, 0), (1, 0), (7, 0), (7, 1)),
        ((2, 0), (2, 1), (6, 0), (6, 1)),
    )
    RELAYS = (
        ((1, 1, 6), (2, 1, 6)),
        ((3, 0, 2), (3, 1, 2)),
        ((0, 0, 2), (1, 1, 2)),
        ((0, 1, 6), (1, 1, 6)),
        ((3, 0, 2), (2, 0, 2), (3, 1, 2)),
        (),
        ((0, 1, 6),),
        ((1, 0, 2), (2, 1, 2)),
    )

    def __init__(self, at, src, buf, sems):
        self.at, self.src, self.buf = at, src, buf
        self.half, self.width = src.shape[0] // 2, src.shape[1]
        self.send, self.recv = sems

    def view(self, slot, half):
        column = slot // 2 * self.width
        return self.buf.at[slot % 2, pl.ds(half * self.half, self.half), pl.ds(column, self.width)]

    def own(self, half):
        return self.src.at[pl.ds(half * self.half, self.half), :]

    def out(self, z, i):
        go, half = self.SENDS[z][i]
        slot = z % 4
        return remote(
            self.own(half), self.view(slot, half), self.send.at[i], self.recv.at[slot, half], self.at.at(z=z + go)
        )

    def keep(self, z, half):
        slot = z % 4
        return pltpu.make_async_copy(self.own(half), self.view(slot, half), self.recv.at[slot, half])

    def came(self, slot, half):
        ref = self.view(slot, half)
        pltpu.make_async_copy(ref, ref, self.recv.at[slot, half]).wait()

    def forward(self, z, i):
        slot, half, go = self.RELAYS[z][i]
        ref = self.view(slot, half)
        return remote(
            ref, ref, self.send.at[len(self.SENDS[z]) + i], self.recv.at[slot, half], self.at.at(z=z + go)
        )

    def each(self, body):
        for z in range(8):
            pl.when(self.at.z == z)(functools.partial(body, z))

    def start(self):
        def body(z):
            for i in range(len(self.SENDS[z])):
                self.out(z, i).start()
            if z % 2 == z // 4:
                for half in (0, 1):
                    self.keep(z, half).start()

        self.each(body)

    def relay(self, turns=(0, 1, 2)):
        def body(z):
            for i, (slot, half, _) in enumerate(self.RELAYS[z]):
                if i in turns:
                    self.came(slot, half)
                    self.forward(z, i).start()

        self.each(body)

    def ready(self, slots=(0, 1, 2, 3)):
        def body(z):
            taken = [(slot, half) for slot, half, _ in self.RELAYS[z]]
            for slot in slots:
                for half in (0, 1):
                    if (slot, half) not in taken:
                        self.came(slot, half)

        self.each(body)

    def drain(self):
        def body(z):
            for i in range(len(self.SENDS[z])):
                self.out(z, i).wait_send()
            for i in range(len(self.RELAYS[z])):
                self.forward(z, i).wait_send()

        self.each(body)


class Foreign:
    def __init__(self, at, tile, buf, sems):
        self.at, self.tile, self.buf = at, tile, buf
        self.rows, self.cols = tile.shape
        (self.sz, self.rz, self.sx, self.rx, self.sf, self.rf, self.sy, self.ry, self.sg, self.rg, self.sc, self.rc) = sems
        self.turn = 1 - 2 * at.core

    def piece(self, x, y, zl=None, whole=False):
        zl = 1 - self.at.zl if zl is None else zl
        count = self.rows if whole else self.rows // 4
        first = (zl * 4 + (x + 4) % 4) * self.rows + (0 if whole else (y + 4) % 4 * count)
        half = self.cols // 2
        return self.buf.at[
            pl.ds(pl.multiple_of(first, 16), count), pl.ds(pl.multiple_of(self.at.core * half, 128), half)
        ]

    def z1(self):
        a, count, half = self.at, self.rows // 4, self.cols // 2
        own = self.tile.at[
            pl.ds(pl.multiple_of(a.y * count, 16), count), pl.ds(pl.multiple_of(a.core * half, 128), half)
        ]
        to = a.at(z=a.zh * 2 + 1 - a.zl)
        return remote(own, self.piece(a.x, a.y, a.zl), self.sz, self.rz, to)

    def x1(self, side):
        a = self.at
        ref = self.piece(a.x, a.y)
        to = a.x + 1 if side == 0 else a.x + 3
        return remote(ref, ref, self.sx.at[side], self.rx.at[side], a.at(x=to))

    def x2(self):
        a = self.at
        ref = self.piece(a.x - self.turn, a.y)
        return remote(ref, ref, self.sf, self.rf, a.at(x=a.x + self.turn + 4))

    def y1(self, side, t):
        a = self.at
        ref = self.piece(a.x + t, a.y)
        to = a.y + 1 if side == 0 else a.y + 3
        return remote(ref, ref, self.sy.at[side, t], self.ry.at[side, t], a.at(y=to))

    def y2(self, t):
        a = self.at
        ref = self.piece(a.x + t, a.y - self.turn)
        return remote(ref, ref, self.sg.at[t], self.rg.at[t], a.at(y=a.y + self.turn + 4))

    def c1(self, t):
        a = self.at
        ref = self.piece(a.x + t, 0, whole=True)
        return remote(ref, ref, self.sc.at[t], self.rc.at[t], a.at(core=1 - a.core))

    def start(self):
        self.z1().start()

    def along(self):
        self.z1().wait_recv()
        for side in (0, 1):
            self.x1(side).start()

    def far(self):
        for side in (0, 1):
            self.x1(side).wait_recv()
        self.x2().start()
        for t in (0, 1, 3):
            for side in (0, 1):
                self.y1(side, t).start()

    def last(self):
        self.x2().wait_recv()
        for side in (0, 1):
            self.y1(side, 2).start()

    def across(self):
        for t in (0, 1, 3, 2):
            for side in (0, 1):
                self.y1(side, t).wait_recv()
            self.y2(t).start()

    def share(self):
        for t in (0, 1, 3, 2):
            self.y2(t).wait_recv()
            self.c1(t).start()

    def ready(self):
        for t in range(4):
            self.c1(t).wait_recv()

    def drain(self):
        self.z1().wait_send()
        self.x2().wait_send()
        for side in (0, 1):
            self.x1(side).wait_send()
            for t in range(4):
                self.y1(side, t).wait_send()
        for t in range(4):
            self.y2(t).wait_send()
            self.c1(t).wait_send()


class Ring:
    def __init__(self, at, buf, sems):
        self.at, self.buf = at, buf
        self.half, self.width = buf.shape[0] // 2, buf.shape[1] // 4
        self.send, self.recv, self.relay_send = sems

    def view(self, place, half):
        column = pl.multiple_of((place + 4) % 4 * self.width, 128)
        return self.buf.at[pl.ds(half * self.half, self.half), pl.ds(column, self.width)]

    def copy(self, place, half, side, send):
        ref = self.view(place, half)
        to = self.at.z + 2 if side == 0 else self.at.z + 6
        return remote(ref, ref, send, self.recv.at[(place + 4) % 4, half], self.at.at(z=to))

    def out(self, side, half):
        return self.copy(self.at.zh, half, side, self.send.at[side, half])

    def forward(self, side):
        place = self.at.zh - 1 if side == 0 else self.at.zh + 1
        return self.copy(place, side, side, self.relay_send.at[side])

    def came(self, place, half):
        ref = self.view(place, half)
        pltpu.make_async_copy(ref, ref, self.recv.at[(place + 4) % 4, half]).wait()

    def start(self):
        for side, half in ((0, 0), (1, 1), (0, 1), (1, 0)):
            self.out(side, half).start()

    def relay(self):
        self.came(self.at.zh - 1, 0)
        self.forward(0).start()
        self.came(self.at.zh + 1, 1)
        self.forward(1).start()

    def ready(self):
        self.came(self.at.zh - 1, 1)
        self.came(self.at.zh + 1, 0)
        self.came(self.at.zh + 2, 0)
        self.came(self.at.zh + 2, 1)

    def drain(self):
        for side in (0, 1):
            for half in (0, 1):
                self.out(side, half).wait_send()
            self.forward(side).wait_send()


def bucket_rows(pick, table):
    first = table.astype(jnp.bfloat16)
    rest = table - first.astype(jnp.float32)
    second = rest.astype(jnp.bfloat16)
    third = (rest - second.astype(jnp.float32)).astype(jnp.bfloat16)
    terms = jnp.concatenate([first, second, third], axis=0)
    return jnp.dot(pick, terms, preferred_element_type=jnp.float32)


def block_kernel(
    tokens_in, ids_in, clips_in, shift_in, scale_in, gate_in, wq, wo, qg_in, kg_in, out,
    tokens, ids, their_ids, clips, shift, scale, gate, qg, kg, cosine, sine, mask, result, in_sem, out_sem, id_sem,
    wq_all, wo_all, raw, a1, a2, row_a, row_b, row_gate, stat_in, stat_col, stats,
    home1, mine1, theirs1, acc1,
    stat_send, stat_recv, c1_send, c1_recv,
    qs0, qs1, qs2, qs3, qs4, qs5, qs6, qs7, qs8,
    os0, os1, os2, os3, os4, os5, os6, os7, os8,
    as0, as1, bs0, bs1, bs2,
    fs0, fs1, fs2, fs3, fs4, fs5, fs6, fs7, fs8, fs9, fs10, fs11,
):
    at = Place()
    wide = tokens.shape[1]
    heads = qg.shape[0] // HD
    buckets = shift.shape[0]
    here = pl.ds(pl.multiple_of(at.zl * (2 * wide), 128), 2 * wide)
    loads = [
        pltpu.make_async_copy(src, dst, in_sem.at[i])
        for i, (src, dst) in enumerate(
            [
                (tokens_in, tokens), (ids_in, ids), (scale_in.at[:, here], scale),
                (shift_in.at[:, here], shift), (gate_in, gate), (clips_in, clips),
                (qg_in, qg), (kg_in, kg),
            ]
        )
    ]
    for load in loads:
        load.start()

    barrier = pltpu.get_barrier_semaphore()
    friends = [at.at(z=at.z + o) for o in range(1, 8)]
    friends += [at.at(x=at.x + 1), at.at(x=at.x + 3), at.at(y=at.y + 1), at.at(y=at.y + 3)]
    friends += [at.at(core=1 - at.core)]
    for friend in friends:
        pl.semaphore_signal(barrier, inc=1, device_id=friend, device_id_type=MESH)
    pl.semaphore_wait(barrier, len(friends))

    qkv = Weights(at, wq, wq_all, (qs0, qs1, qs2, qs3, qs4, qs5, qs6, qs7, qs8), False)
    proj = Weights(at, wo, wo_all, (os0, os1, os2, os3, os4, os5, os6, os7, os8), True, at.zl * 4 * wo.shape[0])
    one = Spread(at, tokens_in, raw, (as0, as1))
    two = Ring(at, a2, (bs0, bs1, bs2))
    other = Foreign(at, wo, wo_all, (fs0, fs1, fs2, fs3, fs4, fs5, fs6, fs7, fs8, fs9, fs10, fs11))

    partner = at.at(z=at.zh * 2 + 1 - at.zl)
    loads[1].wait()
    id_copy = remote(ids, their_ids, id_sem.at[0], id_sem.at[1], partner)
    id_copy.start()
    other.start()
    one.start()
    qkv.start()
    for i, load in enumerate(loads):
        if i != 1:
            load.wait()

    lane = lax.broadcasted_iota(jnp.int32, (16, HD), 1)

    @pl.loop(0, 8)
    def _(i):
        rows = pl.ds(pl.multiple_of(i * 16, 16), 16)
        part = tokens[rows, :].astype(jnp.float32)
        mean = jnp.sum(part, axis=1, keepdims=True) * (1.0 / wide)
        part = part - mean
        spread = jnp.sum(part * part, axis=1, keepdims=True)
        stat_in[rows, :] = jnp.where(lane == 0, mean, jnp.where(lane == 1, spread, 0.0))

    index = lax.broadcasted_iota(jnp.int32, (HD, HD), 0)
    lanes = lax.broadcasted_iota(jnp.int32, (HD, HD), 1)
    stats[at.z] = stat_in[...].T[0:8, :]

    def stat_copy(o):
        ref = stats.at[at.z]
        return remote(ref, ref, stat_send.at[o - 1], stat_recv.at[o - 1], at.at(z=at.z + o))

    for o in range(1, 8):
        stat_copy(o).start()

    qkv.near()
    one.relay()
    count = clips.shape[1]
    lengths = jnp.broadcast_to(clips[...], (8, count)).astype(jnp.bfloat16)
    before = (
        lax.broadcasted_iota(jnp.int32, (count, count), 0)
        <= lax.broadcasted_iota(jnp.int32, (count, count), 1)
    ).astype(jnp.bfloat16)
    ends = jnp.dot(lengths, before, preferred_element_type=jnp.float32)[0:1, :]
    first = (at.zl * 4 + at.x) * 8 + at.y * 2 + at.core
    token = (first * HD + lax.broadcasted_iota(jnp.int32, (HD, count), 0)).astype(jnp.float32)
    passed = ends <= token
    clip = jnp.sum(jnp.where(passed, 1.0, 0.0), axis=1, keepdims=True)
    begin = jnp.sum(jnp.where(passed, clips[...].astype(jnp.float32), 0.0), axis=1, keepdims=True)
    clip = jnp.broadcast_to(clip, (HD, HD))
    mask[...] = jnp.where(clip == clip.T, 1.0, 0.0)
    half = HD // 2
    power = (lanes[:, 0:half]).astype(jnp.float32) * (-math.log(10000.0) / half)
    angles = (token[:, 0:1] - begin) * jnp.exp(power)
    cosine_half, sine_half = jnp.cos(angles), jnp.sin(angles)
    cosine[...] = jnp.concatenate([cosine_half, cosine_half], axis=1)
    sine[...] = jnp.concatenate([-sine_half, sine_half], axis=1)

    def bucket_rows_of(bucket, table):
        bucket = jnp.broadcast_to(bucket[...].astype(jnp.float32), (HD, HD)).T.astype(jnp.int32)
        pick = (bucket[:, 0 : 3 * buckets] == lanes[:, 0 : 3 * buckets] % buckets).astype(jnp.bfloat16)
        return bucket_rows(pick, table[...])

    row_a[at.zl] = 1.0 + bucket_rows_of(ids, scale)
    row_b[at.zl] = bucket_rows_of(ids, shift)
    row_gate[...] = bucket_rows_of(ids, gate)
    id_copy.wait()
    row_a[1 - at.zl] = 1.0 + bucket_rows_of(their_ids, scale)
    row_b[1 - at.zl] = bucket_rows_of(their_ids, shift)

    qkv.far()
    proj.start()
    qkv.across()
    other.along()

    for o in range(1, 8):
        stat_copy(o).wait_recv()

    for block in (0, 1):
        parts = [stats[2 * c + block] for c in range(4)]
        mean = (parts[0][0:1] + parts[1][0:1] + parts[2][0:1] + parts[3][0:1]) * 0.25
        total = jnp.zeros_like(mean)
        for part in parts:
            apart = part[0:1] - mean
            total = total + part[1:2] + wide * (apart * apart)
        rstd = lax.rsqrt(total * (1.0 / (4 * wide)) + EPS)
        stat_col[block] = jnp.where(index == 0, mean, jnp.where(index == 1, rstd, 0.0)).T

    for slot in range(4):
        one.ready((slot,))
        block, part = slot % 2, pl.ds(slot // 2 * wide, wide)

        @pl.loop(0, 8)
        def _(i):
            rows = pl.ds(pl.multiple_of(i * 16, 16), 16)
            normed = raw[block, rows, part].astype(jnp.float32) - stat_col[block, rows, 0:1]
            normed = normed * stat_col[block, rows, 1:2]
            a1[block, rows, part] = (normed * row_a[block, rows, part] + row_b[block, rows, part]).astype(
                jnp.bfloat16
            )

    other.far()
    qkv.ready()

    pieces, piece = result.shape[0], result.shape[2]
    own_rows = pl.ds(pl.multiple_of(at.zl * HD, HD), HD)
    other_rows = pl.ds(pl.multiple_of((1 - at.zl) * HD, HD), HD)

    def swap1(h):
        return remote(mine1.at[h], theirs1.at[h], c1_send.at[h], c1_recv.at[h], partner)

    def store(n):
        columns = pl.ds(pl.multiple_of(n * piece, HD), piece)
        return pltpu.make_async_copy(result.at[n], out.at[:, columns], out_sem.at[n])

    @pl.loop(0, heads)
    def _(h):
        columns = pl.ds(pl.multiple_of(h * (3 * HD), HD), 3 * HD)
        left = a1[...].reshape(2 * HD, a1.shape[2])
        acc1[...] = jnp.dot(left, wq_all[:, columns], preferred_element_type=jnp.float32)
        mine1[h] = acc1[other_rows, :].astype(jnp.bfloat16)
        swap1(h).start()
        home1[h] = acc1[own_rows, :]

    proj.near()
    other.last()

    def rotate(vectors, gains):
        power = jnp.mean(vectors * vectors, axis=-1, keepdims=True)
        vectors = vectors * lax.rsqrt(power + EPS) * gains
        turned = pltpu.roll(vectors, HD // 2, axis=1)
        return (vectors * cosine[...] + turned * sine[...]).astype(jnp.bfloat16)

    @pl.loop(0, heads)
    def _(h):
        swap1(h).wait_recv()
        head = pl.ds(pl.multiple_of(h * HD, HD), HD)
        joined = home1[h] + theirs1[h].astype(jnp.float32)
        query = rotate(joined[:, 0:HD], qg[head].reshape(1, HD))
        key = rotate(joined[:, HD : 2 * HD], kg[head].reshape(1, HD))
        value = joined[:, 2 * HD : 3 * HD].astype(jnp.bfloat16)
        scores = lax.dot_general(
            query, key, (((1,), (1,)), ((), ())), preferred_element_type=jnp.float32
        ) * (1.0 / math.sqrt(HD))
        raised = jnp.where(mask[...] > 0.0, jnp.exp(scores), 0.0)
        weights = (raised / jnp.sum(raised, axis=-1, keepdims=True)).astype(jnp.bfloat16)
        spot = pl.ds(pl.multiple_of(at.zh * (heads * HD) + h * HD, HD), HD)
        a2[:, spot] = jnp.dot(weights, value, preferred_element_type=jnp.float32).astype(
            jnp.bfloat16
        )

    two.start()
    proj.far()
    other.across()
    two.relay()
    proj.across()
    other.share()
    proj.ready()
    other.ready()
    two.ready()

    @pl.loop(0, pieces)
    def _(n):
        columns = pl.ds(pl.multiple_of(n * piece, HD), piece)
        projected = jnp.dot(a2[...], wo_all[:, columns], preferred_element_type=jnp.float32)
        result[n] = (row_gate[:, columns] * projected).astype(jnp.bfloat16)
        store(n).start()

    qkv.drain()
    proj.drain()
    one.drain()
    two.drain()
    other.drain()
    for o in range(1, 8):
        stat_copy(o).wait_send()

    @pl.loop(0, heads)
    def _(h):
        swap1(h).wait_send()

    @pl.loop(0, pieces)
    def _(n):
        store(n).wait()


def shards(
    tokens, bucket_ids, clip_lengths, shift_table, scale_table, gate_table, w_qkv, q_gain, k_gain, w_out
):
    rows, wide = tokens.shape
    heads = w_qkv.shape[1] // (3 * HD)
    pieces = 5
    piece = wide // pieces
    bf16, f32 = jnp.bfloat16, jnp.float32
    dma = pltpu.SemaphoreType.DMA
    weight_sems = [dma((2, 2)), dma((2, 2)), dma((2,)), dma((2,)), dma((3, 2)), dma((3, 2)), dma((3, 4)), dma((3, 4)), dma]
    ring_sems = [dma((2, 2)), dma((4, 2)), dma((2,))]
    foreign_sems = [dma, dma, dma((2,)), dma((2,)), dma, dma, dma((2, 4)), dma((2, 4))] + [dma((4,))] * 4
    spread_sems = [dma((10,)), dma((4, 2))]
    hbm = pl.BlockSpec(memory_space=pltpu.HBM)
    return pl.pallas_call(
        block_kernel,
        out_shape=jax.ShapeDtypeStruct((rows, wide), bf16),
        in_specs=[hbm] * 10,
        out_specs=hbm,
        scratch_shapes=[
            pltpu.VMEM((rows, wide), bf16),
            pltpu.VMEM((1, rows), jnp.int32),
            pltpu.VMEM((1, rows), jnp.int32),
            pltpu.VMEM((1, clip_lengths.shape[0]), jnp.int32),
            pltpu.VMEM((shift_table.shape[0], 2 * wide), f32),
            pltpu.VMEM((shift_table.shape[0], 2 * wide), f32),
            pltpu.VMEM((shift_table.shape[0], wide), f32),
            pltpu.VMEM((heads * HD,), f32),
            pltpu.VMEM((heads * HD,), f32),
            pltpu.VMEM((rows, HD), f32),
            pltpu.VMEM((rows, HD), f32),
            pltpu.VMEM((rows, rows), f32),
            pltpu.VMEM((pieces, rows, piece), bf16),
            dma((8,)),
            dma((pieces,)),
            dma((2,)),
            pltpu.VMEM((4 * w_qkv.shape[0], w_qkv.shape[1]), bf16),
            pltpu.VMEM((8 * w_out.shape[0], w_out.shape[1]), bf16),
            pltpu.VMEM((2, rows, 2 * wide), bf16),
            pltpu.VMEM((2, rows, 2 * wide), bf16),
            pltpu.VMEM((rows, 4 * heads * HD), bf16),
            pltpu.VMEM((2, rows, 2 * wide), f32),
            pltpu.VMEM((2, rows, 2 * wide), f32),
            pltpu.VMEM((rows, wide), f32),
            pltpu.VMEM((rows, HD), f32),
            pltpu.VMEM((2, rows, HD), f32),
            pltpu.VMEM((8, 8, rows), f32),
            pltpu.VMEM((heads, rows, 3 * HD), f32),
            pltpu.VMEM((heads, rows, 3 * HD), bf16),
            pltpu.VMEM((heads, rows, 3 * HD), bf16),
            pltpu.VMEM((2 * rows, 3 * HD), f32),
            dma((7,)), dma((7,)),
            dma((heads,)), dma((heads,)),
        ]
        + weight_sems + weight_sems + spread_sems + ring_sems + foreign_sems,
        compiler_params=pltpu.CompilerParams(
            collective_id=0, has_side_effects=True, vmem_limit_bytes=60 * 1024 * 1024
        ),
    )(
        tokens, bucket_ids.reshape(1, rows), clip_lengths.reshape(1, -1), shift_table, scale_table, gate_table,
        w_qkv, w_out, q_gain, k_gain,
    )


def solution(mesh):
    in_specs = (
        P(("row", "depth"), "col"),
        P(("row", "depth")),
        P(),
        P(),
        P(),
        P(None, "col"),
        P("row", "col"),
        P("col"),
        P("col"),
        P("row", "col"),
    )
    out_specs = P(("row", "depth"), "col")
    return jax.shard_map(shards, mesh=mesh, in_specs=in_specs, out_specs=out_specs, check_vma=False)
```

```python
import functools
import math

import jax
import jax.numpy as jnp
from jax import lax
from jax.experimental import pallas as pl
from jax.experimental.pallas import tpu as pltpu
from jax.sharding import PartitionSpec as P

HD = 128
EPS = 1e-06
MESH = pl.DeviceIdType.MESH


def remote(src, dst, send, recv, device):
    return pltpu.make_async_remote_copy(
        src_ref=src, dst_ref=dst, send_sem=send, recv_sem=recv, device_id=device, device_id_type=MESH
    )


class Place:
    def __init__(self):
        row = lax.axis_index("row")
        depth = lax.axis_index("depth")
        self.zh = lax.axis_index("col")
        self.zl = row // 4
        self.x = row % 4
        self.y = depth // 2
        self.core = depth % 2
        self.z = self.zh * 2 + self.zl

    def at(self, x=None, y=None, z=None, core=None):
        x = self.x if x is None else x % 4
        y = self.y if y is None else y % 4
        z = self.z if z is None else z % 8
        core = self.core if core is None else core
        return ((z % 2) * 4 + x, z // 2, y * 2 + core)


class Weights:
    def __init__(self, at, tile, buf, sems, by_columns, base=0):
        self.at, self.tile, self.buf, self.by_columns, self.base = at, tile, buf, by_columns, base
        self.rows, self.cols = tile.shape
        (self.sx, self.rx, self.sf, self.rf, self.sy, self.ry, self.sc, self.rc, self.own) = sems

    def cut(self, ref, first, quarter, core):
        quarter_rows = self.rows // 4
        if self.by_columns:
            half = self.cols // 2
            return ref.at[
                pl.ds(pl.multiple_of(first + quarter * quarter_rows, 16), quarter_rows),
                pl.ds(pl.multiple_of(core * half, 128), half),
            ]
        half = quarter_rows // 2
        return ref.at[pl.ds(pl.multiple_of(first + quarter * quarter_rows + core * half, 16), half), :]

    def slot(self, x, quarter, core=None):
        core = self.at.core if core is None else core
        return self.cut(self.buf, self.base + (x % 4) * self.rows, quarter % 4, core)

    def x1(self, side, i):
        a = self.at
        to = a.x + 1 if side == 0 else a.x - 1
        return remote(
            self.cut(self.tile, 0, (a.y + i) % 4, a.core),
            self.slot(a.x, a.y + i),
            self.sx.at[side, i],
            self.rx.at[side, i],
            a.at(x=to),
        )

    def x2(self, side):
        a = self.at
        frm = a.x - 1 if side == 0 else a.x + 1
        to = a.x + 1 if side == 0 else a.x - 1
        ref = self.slot(frm, a.y + side)
        return remote(ref, ref, self.sf.at[side], self.rf.at[side], a.at(x=to))

    def y1(self, t, side):
        a = self.at
        ref = self.slot(a.x + t, a.y + side)
        to = a.y + 1 if side == 0 else a.y - 1
        return remote(ref, ref, self.sy.at[t - 1, side], self.ry.at[t - 1, side], a.at(y=to))

    def c1(self, t, i):
        a = self.at
        ref = self.slot(a.x + t, a.y + i)
        return remote(ref, ref, self.sc.at[t - 1, i], self.rc.at[t - 1, i], a.at(core=1 - a.core))

    def local(self):
        first = pl.multiple_of(self.base + self.at.x * self.rows, 16)
        return pltpu.make_async_copy(self.tile, self.buf.at[pl.ds(first, self.rows), :], self.own)

    def start(self):
        for side, i in ((0, 0), (1, 1), (0, 1), (1, 0)):
            self.x1(side, i).start()
        self.local().start()

    def near(self):
        for side in (0, 1):
            t = 3 if side == 0 else 1
            self.x1(side, side).wait_recv()
            self.x2(side).start()
            self.y1(t, side).start()
            self.c1(t, side).start()
        for side in (0, 1):
            t = 3 if side == 0 else 1
            self.x1(side, 1 - side).wait_recv()
            self.y1(t, 1 - side).start()
            self.c1(t, 1 - side).start()

    def far(self):
        for side in (0, 1):
            self.x2(side).wait_recv()
            self.y1(2, side).start()
            self.c1(2, side).start()

    def across(self, tiles=(3, 1, 2)):
        for t in tiles:
            for side in (0, 1):
                self.y1(t, side).wait_recv()
                self.c1(t, 3 if side == 0 else 2).start()

    def ready(self):
        self.local().wait()
        for t in (3, 1, 2):
            for i in range(4):
                self.c1(t, i).wait_recv()

    def drain(self):
        for side in (0, 1):
            for i in (0, 1):
                self.x1(side, i).wait_send()
            self.x2(side).wait_send()
        for t in (1, 2, 3):
            for side in (0, 1):
                self.y1(t, side).wait_send()
            for i in range(4):
                self.c1(t, i).wait_send()


class Spread:
    SENDS = (
        ((2, 0), (6, 1), (2, 1), (6, 0)),
        ((1, 1), (7, 1), (3, 0), (5, 0), (1, 0), (7, 0)),
        ((2, 0), (6, 1), (2, 1), (6, 0)),
        ((1, 0), (1, 1), (5, 0), (5, 1), (7, 0), (7, 1)),
        ((7, 1), (3, 0), (3, 1), (5, 0), (1, 0), (1, 1), (7, 0)),
        ((2, 0), (6, 1), (2, 1), (6, 0)),
        ((1, 1), (5, 0), (5, 1), (3, 0), (1, 0), (7, 0), (7, 1)),
        ((2, 0), (2, 1), (6, 0), (6, 1)),
    )
    RELAYS = (
        ((1, 1, 6), (2, 1, 6)),
        ((3, 0, 2), (3, 1, 2)),
        ((0, 0, 2), (1, 1, 2)),
        ((0, 1, 6), (1, 1, 6)),
        ((3, 0, 2), (2, 0, 2), (3, 1, 2)),
        (),
        ((0, 1, 6),),
        ((1, 0, 2), (2, 1, 2)),
    )

    def __init__(self, at, src, buf, sems):
        self.at, self.src, self.buf = at, src, buf
        self.half, self.width = src.shape[0] // 2, src.shape[1]
        self.send, self.recv = sems

    def view(self, slot, half):
        column = slot // 2 * self.width
        return self.buf.at[slot % 2, pl.ds(half * self.half, self.half), pl.ds(column, self.width)]

    def own(self, half):
        return self.src.at[pl.ds(half * self.half, self.half), :]

    def out(self, z, i):
        go, half = self.SENDS[z][i]
        slot = z % 4
        return remote(
            self.own(half), self.view(slot, half), self.send.at[i], self.recv.at[slot, half], self.at.at(z=z + go)
        )

    def keep(self, z, half):
        slot = z % 4
        return pltpu.make_async_copy(self.own(half), self.view(slot, half), self.recv.at[slot, half])

    def came(self, slot, half):
        ref = self.view(slot, half)
        pltpu.make_async_copy(ref, ref, self.recv.at[slot, half]).wait()

    def forward(self, z, i):
        slot, half, go = self.RELAYS[z][i]
        ref = self.view(slot, half)
        return remote(
            ref, ref, self.send.at[len(self.SENDS[z]) + i], self.recv.at[slot, half], self.at.at(z=z + go)
        )

    def each(self, body):
        for z in range(8):
            pl.when(self.at.z == z)(functools.partial(body, z))

    def start(self):
        def body(z):
            for i in range(len(self.SENDS[z])):
                self.out(z, i).start()
            if z % 2 == z // 4:
                for half in (0, 1):
                    self.keep(z, half).start()

        self.each(body)

    def relay(self, turns=(0, 1, 2)):
        def body(z):
            for i, (slot, half, _) in enumerate(self.RELAYS[z]):
                if i in turns:
                    self.came(slot, half)
                    self.forward(z, i).start()

        self.each(body)

    def ready(self, slots=(0, 1, 2, 3)):
        def body(z):
            taken = [(slot, half) for slot, half, _ in self.RELAYS[z]]
            for slot in slots:
                for half in (0, 1):
                    if (slot, half) not in taken:
                        self.came(slot, half)

        self.each(body)

    def drain(self):
        def body(z):
            for i in range(len(self.SENDS[z])):
                self.out(z, i).wait_send()
            for i in range(len(self.RELAYS[z])):
                self.forward(z, i).wait_send()

        self.each(body)


class Foreign:
    def __init__(self, at, tile, buf, sems):
        self.at, self.tile, self.buf = at, tile, buf
        self.rows, self.cols = tile.shape
        (self.sz, self.rz, self.sx, self.rx, self.sf, self.rf, self.sy, self.ry, self.sg, self.rg, self.sc, self.rc) = sems
        self.turn = 1 - 2 * at.core

    def piece(self, x, y, zl=None, whole=False):
        zl = 1 - self.at.zl if zl is None else zl
        count = self.rows if whole else self.rows // 4
        first = (zl * 4 + (x + 4) % 4) * self.rows + (0 if whole else (y + 4) % 4 * count)
        half = self.cols // 2
        return self.buf.at[
            pl.ds(pl.multiple_of(first, 16), count), pl.ds(pl.multiple_of(self.at.core * half, 128), half)
        ]

    def z1(self):
        a, count, half = self.at, self.rows // 4, self.cols // 2
        own = self.tile.at[
            pl.ds(pl.multiple_of(a.y * count, 16), count), pl.ds(pl.multiple_of(a.core * half, 128), half)
        ]
        to = a.at(z=a.zh * 2 + 1 - a.zl)
        return remote(own, self.piece(a.x, a.y, a.zl), self.sz, self.rz, to)

    def x1(self, side):
        a = self.at
        ref = self.piece(a.x, a.y)
        to = a.x + 1 if side == 0 else a.x + 3
        return remote(ref, ref, self.sx.at[side], self.rx.at[side], a.at(x=to))

    def x2(self):
        a = self.at
        ref = self.piece(a.x - self.turn, a.y)
        return remote(ref, ref, self.sf, self.rf, a.at(x=a.x + self.turn + 4))

    def y1(self, side, t):
        a = self.at
        ref = self.piece(a.x + t, a.y)
        to = a.y + 1 if side == 0 else a.y + 3
        return remote(ref, ref, self.sy.at[side, t], self.ry.at[side, t], a.at(y=to))

    def y2(self, t):
        a = self.at
        ref = self.piece(a.x + t, a.y - self.turn)
        return remote(ref, ref, self.sg.at[t], self.rg.at[t], a.at(y=a.y + self.turn + 4))

    def c1(self, t):
        a = self.at
        ref = self.piece(a.x + t, 0, whole=True)
        return remote(ref, ref, self.sc.at[t], self.rc.at[t], a.at(core=1 - a.core))

    def start(self):
        self.z1().start()

    def along(self):
        self.z1().wait_recv()
        for side in (0, 1):
            self.x1(side).start()

    def far(self):
        for side in (0, 1):
            self.x1(side).wait_recv()
        self.x2().start()
        for t in (0, 1, 3):
            for side in (0, 1):
                self.y1(side, t).start()

    def last(self):
        self.x2().wait_recv()
        for side in (0, 1):
            self.y1(side, 2).start()

    def across(self):
        for t in (0, 1, 3, 2):
            for side in (0, 1):
                self.y1(side, t).wait_recv()
            self.y2(t).start()

    def share(self):
        for t in (0, 1, 3, 2):
            self.y2(t).wait_recv()
            self.c1(t).start()

    def ready(self):
        for t in range(4):
            self.c1(t).wait_recv()

    def drain(self):
        self.z1().wait_send()
        self.x2().wait_send()
        for side in (0, 1):
            self.x1(side).wait_send()
            for t in range(4):
                self.y1(side, t).wait_send()
        for t in range(4):
            self.y2(t).wait_send()
            self.c1(t).wait_send()


class Ring:
    def __init__(self, at, buf, sems):
        self.at, self.buf = at, buf
        self.half, self.width = buf.shape[0] // 2, buf.shape[1] // 4
        self.send, self.recv, self.relay_send = sems

    def view(self, place, half):
        column = pl.multiple_of((place + 4) % 4 * self.width, 128)
        return self.buf.at[pl.ds(half * self.half, self.half), pl.ds(column, self.width)]

    def copy(self, place, half, side, send):
        ref = self.view(place, half)
        to = self.at.z + 2 if side == 0 else self.at.z + 6
        return remote(ref, ref, send, self.recv.at[(place + 4) % 4, half], self.at.at(z=to))

    def out(self, side, half):
        return self.copy(self.at.zh, half, side, self.send.at[side, half])

    def forward(self, side):
        place = self.at.zh - 1 if side == 0 else self.at.zh + 1
        return self.copy(place, side, side, self.relay_send.at[side])

    def came(self, place, half):
        ref = self.view(place, half)
        pltpu.make_async_copy(ref, ref, self.recv.at[(place + 4) % 4, half]).wait()

    def start(self):
        for side, half in ((0, 0), (1, 1), (0, 1), (1, 0)):
            self.out(side, half).start()

    def relay(self):
        self.came(self.at.zh - 1, 0)
        self.forward(0).start()
        self.came(self.at.zh + 1, 1)
        self.forward(1).start()

    def ready(self):
        self.came(self.at.zh - 1, 1)
        self.came(self.at.zh + 1, 0)
        self.came(self.at.zh + 2, 0)
        self.came(self.at.zh + 2, 1)

    def drain(self):
        for side in (0, 1):
            for half in (0, 1):
                self.out(side, half).wait_send()
            self.forward(side).wait_send()


def bucket_rows(pick, table):
    first = table.astype(jnp.bfloat16)
    rest = table - first.astype(jnp.float32)
    second = rest.astype(jnp.bfloat16)
    third = (rest - second.astype(jnp.float32)).astype(jnp.bfloat16)
    terms = jnp.concatenate([first, second, third], axis=0)
    return jnp.dot(pick, terms, preferred_element_type=jnp.float32)


def block_kernel(
    tokens_in, ids_in, clips_in, shift_in, scale_in, gate_in, wq, wo, qg_in, kg_in, out,
    tokens, ids, their_ids, clips, shift, scale, gate, qg, kg, cosine, sine, mask, result, in_sem, out_sem, id_sem,
    wq_all, wo_all, raw, a1, a2, row_a, row_b, row_gate, stat_in, stat_col, stats,
    home1, mine1, theirs1, acc1,
    stat_send, stat_recv, c1_send, c1_recv,
    qs0, qs1, qs2, qs3, qs4, qs5, qs6, qs7, qs8,
    os0, os1, os2, os3, os4, os5, os6, os7, os8,
    as0, as1, bs0, bs1, bs2,
    fs0, fs1, fs2, fs3, fs4, fs5, fs6, fs7, fs8, fs9, fs10, fs11,
):
    at = Place()
    wide = tokens.shape[1]
    heads = qg.shape[0] // HD
    buckets = shift.shape[0]
    here = pl.ds(pl.multiple_of(at.zl * (2 * wide), 128), 2 * wide)
    loads = [
        pltpu.make_async_copy(src, dst, in_sem.at[i])
        for i, (src, dst) in enumerate(
            [
                (tokens_in, tokens), (ids_in, ids), (scale_in.at[:, here], scale),
                (shift_in.at[:, here], shift), (gate_in, gate), (clips_in, clips),
                (qg_in, qg), (kg_in, kg),
            ]
        )
    ]
    for load in loads:
        load.start()

    barrier = pltpu.get_barrier_semaphore()
    friends = [at.at(z=at.z + o) for o in range(1, 8)]
    friends += [at.at(x=at.x + 1), at.at(x=at.x + 3), at.at(y=at.y + 1), at.at(y=at.y + 3)]
    friends += [at.at(core=1 - at.core)]
    for friend in friends:
        pl.semaphore_signal(barrier, inc=1, device_id=friend, device_id_type=MESH)
    pl.semaphore_wait(barrier, len(friends))

    qkv = Weights(at, wq, wq_all, (qs0, qs1, qs2, qs3, qs4, qs5, qs6, qs7, qs8), False)
    proj = Weights(at, wo, wo_all, (os0, os1, os2, os3, os4, os5, os6, os7, os8), True, at.zl * 4 * wo.shape[0])
    one = Spread(at, tokens_in, raw, (as0, as1))
    two = Ring(at, a2, (bs0, bs1, bs2))
    other = Foreign(at, wo, wo_all, (fs0, fs1, fs2, fs3, fs4, fs5, fs6, fs7, fs8, fs9, fs10, fs11))

    partner = at.at(z=at.zh * 2 + 1 - at.zl)
    loads[1].wait()
    id_copy = remote(ids, their_ids, id_sem.at[0], id_sem.at[1], partner)
    id_copy.start()
    other.start()
    one.start()
    qkv.start()
    for i, load in enumerate(loads):
        if i != 1:
            load.wait()

    lane = lax.broadcasted_iota(jnp.int32, (16, HD), 1)

    @pl.loop(0, 8)
    def _(i):
        rows = pl.ds(pl.multiple_of(i * 16, 16), 16)
        part = tokens[rows, :].astype(jnp.float32)
        mean = jnp.sum(part, axis=1, keepdims=True) * (1.0 / wide)
        part = part - mean
        spread = jnp.sum(part * part, axis=1, keepdims=True)
        stat_in[rows, :] = jnp.where(lane == 0, mean, jnp.where(lane == 1, spread, 0.0))

    index = lax.broadcasted_iota(jnp.int32, (HD, HD), 0)
    lanes = lax.broadcasted_iota(jnp.int32, (HD, HD), 1)
    stats[at.z] = stat_in[...].T[0:8, :]

    def stat_copy(o):
        ref = stats.at[at.z]
        return remote(ref, ref, stat_send.at[o - 1], stat_recv.at[o - 1], at.at(z=at.z + o))

    for o in range(1, 8):
        stat_copy(o).start()

    qkv.near()
    one.relay((0,))
    count = clips.shape[1]
    lengths = jnp.broadcast_to(clips[...], (8, count)).astype(jnp.bfloat16)
    before = (
        lax.broadcasted_iota(jnp.int32, (count, count), 0)
        <= lax.broadcasted_iota(jnp.int32, (count, count), 1)
    ).astype(jnp.bfloat16)
    ends = jnp.dot(lengths, before, preferred_element_type=jnp.float32)[0:1, :]
    first = (at.zl * 4 + at.x) * 8 + at.y * 2 + at.core
    token = (first * HD + lax.broadcasted_iota(jnp.int32, (HD, count), 0)).astype(jnp.float32)
    passed = ends <= token
    clip = jnp.sum(jnp.where(passed, 1.0, 0.0), axis=1, keepdims=True)
    begin = jnp.sum(jnp.where(passed, clips[...].astype(jnp.float32), 0.0), axis=1, keepdims=True)
    clip = jnp.broadcast_to(clip, (HD, HD))
    mask[...] = jnp.where(clip == clip.T, 1.0, 0.0)
    half = HD // 2
    power = (lanes[:, 0:half]).astype(jnp.float32) * (-math.log(10000.0) / half)
    angles = (token[:, 0:1] - begin) * jnp.exp(power)
    cosine_half, sine_half = jnp.cos(angles), jnp.sin(angles)
    cosine[...] = jnp.concatenate([cosine_half, cosine_half], axis=1)
    sine[...] = jnp.concatenate([-sine_half, sine_half], axis=1)

    def bucket_rows_of(bucket, table):
        bucket = jnp.broadcast_to(bucket[...].astype(jnp.float32), (HD, HD)).T.astype(jnp.int32)
        pick = (bucket[:, 0 : 3 * buckets] == lanes[:, 0 : 3 * buckets] % buckets).astype(jnp.bfloat16)
        return bucket_rows(pick, table[...])

    row_a[at.zl] = 1.0 + bucket_rows_of(ids, scale)
    row_b[at.zl] = bucket_rows_of(ids, shift)
    row_gate[...] = bucket_rows_of(ids, gate)
    id_copy.wait()
    row_a[1 - at.zl] = 1.0 + bucket_rows_of(their_ids, scale)
    row_b[1 - at.zl] = bucket_rows_of(their_ids, shift)

    qkv.far()
    one.relay((1, 2))
    proj.start()
    qkv.across((3, 1))
    for o in range(1, 8):
        stat_copy(o).wait_recv()

    for block in (0, 1):
        parts = [stats[2 * c + block] for c in range(4)]
        mean = (parts[0][0:1] + parts[1][0:1] + parts[2][0:1] + parts[3][0:1]) * 0.25
        total = jnp.zeros_like(mean)
        for part in parts:
            apart = part[0:1] - mean
            total = total + part[1:2] + wide * (apart * apart)
        rstd = lax.rsqrt(total * (1.0 / (4 * wide)) + EPS)
        stat_col[block] = jnp.where(index == 0, mean, jnp.where(index == 1, rstd, 0.0)).T

    qkv.across((2,))
    other.along()
    for slot in range(4):
        one.ready((slot,))
        block, part = slot % 2, pl.ds(slot // 2 * wide, wide)

        @pl.loop(0, 8)
        def _(i):
            rows = pl.ds(pl.multiple_of(i * 16, 16), 16)
            normed = raw[block, rows, part].astype(jnp.float32) - stat_col[block, rows, 0:1]
            normed = normed * stat_col[block, rows, 1:2]
            a1[block, rows, part] = (normed * row_a[block, rows, part] + row_b[block, rows, part]).astype(
                jnp.bfloat16
            )

    qkv.ready()
    other.far()

    pieces, piece = result.shape[0], result.shape[2]
    own_rows = pl.ds(pl.multiple_of(at.zl * HD, HD), HD)
    other_rows = pl.ds(pl.multiple_of((1 - at.zl) * HD, HD), HD)

    def swap1(h):
        return remote(mine1.at[h], theirs1.at[h], c1_send.at[h], c1_recv.at[h], partner)

    def store(n):
        columns = pl.ds(pl.multiple_of(n * piece, HD), piece)
        return pltpu.make_async_copy(result.at[n], out.at[:, columns], out_sem.at[n])

    @pl.loop(0, heads)
    def _(h):
        columns = pl.ds(pl.multiple_of(h * (3 * HD), HD), 3 * HD)
        left = a1[...].reshape(2 * HD, a1.shape[2])
        acc1[...] = jnp.dot(left, wq_all[:, columns], preferred_element_type=jnp.float32)
        mine1[h] = acc1[other_rows, :].astype(jnp.bfloat16)
        swap1(h).start()
        home1[h] = acc1[own_rows, :]

    proj.near()
    other.last()

    def rotate(vectors, gains):
        power = jnp.mean(vectors * vectors, axis=-1, keepdims=True)
        vectors = vectors * lax.rsqrt(power + EPS) * gains
        turned = pltpu.roll(vectors, HD // 2, axis=1)
        return (vectors * cosine[...] + turned * sine[...]).astype(jnp.bfloat16)

    @pl.loop(0, heads)
    def _(h):
        swap1(h).wait_recv()
        head = pl.ds(pl.multiple_of(h * HD, HD), HD)
        joined = home1[h] + theirs1[h].astype(jnp.float32)
        query = rotate(joined[:, 0:HD], qg[head].reshape(1, HD))
        key = rotate(joined[:, HD : 2 * HD], kg[head].reshape(1, HD))
        value = joined[:, 2 * HD : 3 * HD].astype(jnp.bfloat16)
        scores = lax.dot_general(
            query, key, (((1,), (1,)), ((), ())), preferred_element_type=jnp.float32
        ) * (1.0 / math.sqrt(HD))
        raised = jnp.where(mask[...] > 0.0, jnp.exp(scores), 0.0)
        weights = (raised / jnp.sum(raised, axis=-1, keepdims=True)).astype(jnp.bfloat16)
        spot = pl.ds(pl.multiple_of(at.zh * (heads * HD) + h * HD, HD), HD)
        a2[:, spot] = jnp.dot(weights, value, preferred_element_type=jnp.float32).astype(
            jnp.bfloat16
        )

    two.start()
    proj.far()
    other.across()
    two.relay()
    proj.across()
    other.share()
    proj.ready()
    other.ready()
    two.ready()

    @pl.loop(0, pieces)
    def _(n):
        columns = pl.ds(pl.multiple_of(n * piece, HD), piece)
        projected = jnp.dot(a2[...], wo_all[:, columns], preferred_element_type=jnp.float32)
        result[n] = (row_gate[:, columns] * projected).astype(jnp.bfloat16)
        store(n).start()

    qkv.drain()
    proj.drain()
    one.drain()
    two.drain()
    other.drain()
    for o in range(1, 8):
        stat_copy(o).wait_send()

    @pl.loop(0, heads)
    def _(h):
        swap1(h).wait_send()

    @pl.loop(0, pieces)
    def _(n):
        store(n).wait()


def shards(
    tokens, bucket_ids, clip_lengths, shift_table, scale_table, gate_table, w_qkv, q_gain, k_gain, w_out
):
    rows, wide = tokens.shape
    heads = w_qkv.shape[1] // (3 * HD)
    pieces = 5
    piece = wide // pieces
    bf16, f32 = jnp.bfloat16, jnp.float32
    dma = pltpu.SemaphoreType.DMA
    weight_sems = [dma((2, 2)), dma((2, 2)), dma((2,)), dma((2,)), dma((3, 2)), dma((3, 2)), dma((3, 4)), dma((3, 4)), dma]
    ring_sems = [dma((2, 2)), dma((4, 2)), dma((2,))]
    foreign_sems = [dma, dma, dma((2,)), dma((2,)), dma, dma, dma((2, 4)), dma((2, 4))] + [dma((4,))] * 4
    spread_sems = [dma((10,)), dma((4, 2))]
    hbm = pl.BlockSpec(memory_space=pltpu.HBM)
    return pl.pallas_call(
        block_kernel,
        out_shape=jax.ShapeDtypeStruct((rows, wide), bf16),
        in_specs=[hbm] * 10,
        out_specs=hbm,
        scratch_shapes=[
            pltpu.VMEM((rows, wide), bf16),
            pltpu.VMEM((1, rows), jnp.int32),
            pltpu.VMEM((1, rows), jnp.int32),
            pltpu.VMEM((1, clip_lengths.shape[0]), jnp.int32),
            pltpu.VMEM((shift_table.shape[0], 2 * wide), f32),
            pltpu.VMEM((shift_table.shape[0], 2 * wide), f32),
            pltpu.VMEM((shift_table.shape[0], wide), f32),
            pltpu.VMEM((heads * HD,), f32),
            pltpu.VMEM((heads * HD,), f32),
            pltpu.VMEM((rows, HD), f32),
            pltpu.VMEM((rows, HD), f32),
            pltpu.VMEM((rows, rows), f32),
            pltpu.VMEM((pieces, rows, piece), bf16),
            dma((8,)),
            dma((pieces,)),
            dma((2,)),
            pltpu.VMEM((4 * w_qkv.shape[0], w_qkv.shape[1]), bf16),
            pltpu.VMEM((8 * w_out.shape[0], w_out.shape[1]), bf16),
            pltpu.VMEM((2, rows, 2 * wide), bf16),
            pltpu.VMEM((2, rows, 2 * wide), bf16),
            pltpu.VMEM((rows, 4 * heads * HD), bf16),
            pltpu.VMEM((2, rows, 2 * wide), f32),
            pltpu.VMEM((2, rows, 2 * wide), f32),
            pltpu.VMEM((rows, wide), f32),
            pltpu.VMEM((rows, HD), f32),
            pltpu.VMEM((2, rows, HD), f32),
            pltpu.VMEM((8, 8, rows), f32),
            pltpu.VMEM((heads, rows, 3 * HD), f32),
            pltpu.VMEM((heads, rows, 3 * HD), bf16),
            pltpu.VMEM((heads, rows, 3 * HD), bf16),
            pltpu.VMEM((2 * rows, 3 * HD), f32),
            dma((7,)), dma((7,)),
            dma((heads,)), dma((heads,)),
        ]
        + weight_sems + weight_sems + spread_sems + ring_sems + foreign_sems,
        compiler_params=pltpu.CompilerParams(
            collective_id=0, has_side_effects=True, vmem_limit_bytes=60 * 1024 * 1024
        ),
    )(
        tokens, bucket_ids.reshape(1, rows), clip_lengths.reshape(1, -1), shift_table, scale_table, gate_table,
        w_qkv, w_out, q_gain, k_gain,
    )


def solution(mesh):
    in_specs = (
        P(("row", "depth"), "col"),
        P(("row", "depth")),
        P(),
        P(),
        P(),
        P(None, "col"),
        P("row", "col"),
        P("col"),
        P("col"),
        P("row", "col"),
    )
    out_specs = P(("row", "depth"), "col")
    return jax.shard_map(shards, mesh=mesh, in_specs=in_specs, out_specs=out_specs, check_vma=False)
```

```python
import functools
import math

import jax
import jax.numpy as jnp
from jax import lax
from jax.experimental import pallas as pl
from jax.experimental.pallas import tpu as pltpu
from jax.sharding import PartitionSpec as P

HD = 128
EPS = 1e-06
MESH = pl.DeviceIdType.MESH


def remote(src, dst, send, recv, device):
    return pltpu.make_async_remote_copy(
        src_ref=src, dst_ref=dst, send_sem=send, recv_sem=recv, device_id=device, device_id_type=MESH
    )


class Place:
    def __init__(self):
        row = lax.axis_index("row")
        depth = lax.axis_index("depth")
        self.zh = lax.axis_index("col")
        self.zl = row // 4
        self.x = row % 4
        self.y = depth // 2
        self.core = depth % 2
        self.z = self.zh * 2 + self.zl

    def at(self, x=None, y=None, z=None, core=None):
        x = self.x if x is None else x % 4
        y = self.y if y is None else y % 4
        z = self.z if z is None else z % 8
        core = self.core if core is None else core
        return ((z % 2) * 4 + x, z // 2, y * 2 + core)


class Weights:
    def __init__(self, at, tile, buf, sems, by_columns, base=0):
        self.at, self.tile, self.buf, self.by_columns, self.base = at, tile, buf, by_columns, base
        self.rows, self.cols = tile.shape
        (self.sx, self.rx, self.sf, self.rf, self.sy, self.ry, self.sc, self.rc, self.own) = sems

    def cut(self, ref, first, quarter, core):
        quarter_rows = self.rows // 4
        if self.by_columns:
            half = self.cols // 2
            return ref.at[
                pl.ds(pl.multiple_of(first + quarter * quarter_rows, 16), quarter_rows),
                pl.ds(pl.multiple_of(core * half, 128), half),
            ]
        half = quarter_rows // 2
        return ref.at[pl.ds(pl.multiple_of(first + quarter * quarter_rows + core * half, 16), half), :]

    def slot(self, x, quarter, core=None):
        core = self.at.core if core is None else core
        return self.cut(self.buf, self.base + (x % 4) * self.rows, quarter % 4, core)

    def x1(self, side, i):
        a = self.at
        to = a.x + 1 if side == 0 else a.x - 1
        return remote(
            self.cut(self.tile, 0, (a.y + i) % 4, a.core),
            self.slot(a.x, a.y + i),
            self.sx.at[side, i],
            self.rx.at[side, i],
            a.at(x=to),
        )

    def x2(self, side):
        a = self.at
        frm = a.x - 1 if side == 0 else a.x + 1
        to = a.x + 1 if side == 0 else a.x - 1
        ref = self.slot(frm, a.y + side)
        return remote(ref, ref, self.sf.at[side], self.rf.at[side], a.at(x=to))

    def y1(self, t, side):
        a = self.at
        ref = self.slot(a.x + t, a.y + side)
        to = a.y + 1 if side == 0 else a.y - 1
        return remote(ref, ref, self.sy.at[t - 1, side], self.ry.at[t - 1, side], a.at(y=to))

    def c1(self, t, i):
        a = self.at
        ref = self.slot(a.x + t, a.y + i)
        return remote(ref, ref, self.sc.at[t - 1, i], self.rc.at[t - 1, i], a.at(core=1 - a.core))

    def local(self):
        first = pl.multiple_of(self.base + self.at.x * self.rows, 16)
        return pltpu.make_async_copy(self.tile, self.buf.at[pl.ds(first, self.rows), :], self.own)

    def start(self):
        for side, i in ((0, 0), (1, 1), (0, 1), (1, 0)):
            self.x1(side, i).start()
        self.local().start()

    def near(self):
        for side in (0, 1):
            t = 3 if side == 0 else 1
            self.x1(side, side).wait_recv()
            self.x2(side).start()
            self.y1(t, side).start()
            self.c1(t, side).start()
        for side in (0, 1):
            t = 3 if side == 0 else 1
            self.x1(side, 1 - side).wait_recv()
            self.y1(t, 1 - side).start()
            self.c1(t, 1 - side).start()

    def far(self):
        for side in (0, 1):
            self.x2(side).wait_recv()
            self.y1(2, side).start()
            self.c1(2, side).start()

    def across(self, tiles=(3, 1, 2)):
        for t in tiles:
            for side in (0, 1):
                self.y1(t, side).wait_recv()
                self.c1(t, 3 if side == 0 else 2).start()

    def ready(self):
        self.local().wait()
        for t in (3, 1, 2):
            for i in range(4):
                self.c1(t, i).wait_recv()

    def drain(self):
        for side in (0, 1):
            for i in (0, 1):
                self.x1(side, i).wait_send()
            self.x2(side).wait_send()
        for t in (1, 2, 3):
            for side in (0, 1):
                self.y1(t, side).wait_send()
            for i in range(4):
                self.c1(t, i).wait_send()


class Spread:
    SENDS = (
        ((2, 0), (6, 1), (2, 1), (6, 0)),
        ((1, 1), (7, 1), (3, 0), (5, 0), (1, 0), (7, 0)),
        ((2, 0), (6, 1), (2, 1), (6, 0)),
        ((1, 0), (1, 1), (5, 0), (5, 1), (7, 0), (7, 1)),
        ((7, 1), (3, 0), (3, 1), (5, 0), (1, 0), (1, 1), (7, 0)),
        ((2, 0), (6, 1), (2, 1), (6, 0)),
        ((1, 1), (5, 0), (5, 1), (3, 0), (1, 0), (7, 0), (7, 1)),
        ((2, 0), (2, 1), (6, 0), (6, 1)),
    )
    RELAYS = (
        ((1, 1, 6), (2, 1, 6)),
        ((3, 0, 2), (3, 1, 2)),
        ((0, 0, 2), (1, 1, 2)),
        ((0, 1, 6), (1, 1, 6)),
        ((3, 0, 2), (2, 0, 2), (3, 1, 2)),
        (),
        ((0, 1, 6),),
        ((1, 0, 2), (2, 1, 2)),
    )

    def __init__(self, at, src, buf, sems):
        self.at, self.src, self.buf = at, src, buf
        self.half, self.width = src.shape[0] // 2, src.shape[1]
        self.send, self.recv = sems

    def view(self, slot, half):
        column = slot // 2 * self.width
        return self.buf.at[slot % 2, pl.ds(half * self.half, self.half), pl.ds(column, self.width)]

    def own(self, half):
        return self.src.at[pl.ds(half * self.half, self.half), :]

    def out(self, z, i):
        go, half = self.SENDS[z][i]
        slot = z % 4
        return remote(
            self.own(half), self.view(slot, half), self.send.at[i], self.recv.at[slot, half], self.at.at(z=z + go)
        )

    def keep(self, z, half):
        slot = z % 4
        return pltpu.make_async_copy(self.own(half), self.view(slot, half), self.recv.at[slot, half])

    def came(self, slot, half):
        ref = self.view(slot, half)
        pltpu.make_async_copy(ref, ref, self.recv.at[slot, half]).wait()

    def forward(self, z, i):
        slot, half, go = self.RELAYS[z][i]
        ref = self.view(slot, half)
        return remote(
            ref, ref, self.send.at[len(self.SENDS[z]) + i], self.recv.at[slot, half], self.at.at(z=z + go)
        )

    def each(self, body):
        for z in range(8):
            pl.when(self.at.z == z)(functools.partial(body, z))

    def start(self):
        def body(z):
            for i in range(len(self.SENDS[z])):
                self.out(z, i).start()
            if z % 2 == z // 4:
                for half in (0, 1):
                    self.keep(z, half).start()

        self.each(body)

    def relay(self, turns=(0, 1, 2)):
        def body(z):
            for i, (slot, half, _) in enumerate(self.RELAYS[z]):
                if i in turns:
                    self.came(slot, half)
                    self.forward(z, i).start()

        self.each(body)

    def ready(self, slots=(0, 1, 2, 3)):
        def body(z):
            taken = [(slot, half) for slot, half, _ in self.RELAYS[z]]
            for slot in slots:
                for half in (0, 1):
                    if (slot, half) not in taken:
                        self.came(slot, half)

        self.each(body)

    def drain(self):
        def body(z):
            for i in range(len(self.SENDS[z])):
                self.out(z, i).wait_send()
            for i in range(len(self.RELAYS[z])):
                self.forward(z, i).wait_send()

        self.each(body)


class Foreign:
    def __init__(self, at, tile, buf, sems):
        self.at, self.tile, self.buf = at, tile, buf
        self.rows, self.cols = tile.shape
        (self.sz, self.rz, self.sx, self.rx, self.sf, self.rf, self.sy, self.ry, self.sg, self.rg, self.sc, self.rc) = sems
        self.turn = 1 - 2 * at.core

    def piece(self, x, y, zl=None, whole=False):
        zl = 1 - self.at.zl if zl is None else zl
        count = self.rows if whole else self.rows // 4
        first = (zl * 4 + (x + 4) % 4) * self.rows + (0 if whole else (y + 4) % 4 * count)
        half = self.cols // 2
        return self.buf.at[
            pl.ds(pl.multiple_of(first, 16), count), pl.ds(pl.multiple_of(self.at.core * half, 128), half)
        ]

    def z1(self):
        a, count, half = self.at, self.rows // 4, self.cols // 2
        own = self.tile.at[
            pl.ds(pl.multiple_of(a.y * count, 16), count), pl.ds(pl.multiple_of(a.core * half, 128), half)
        ]
        to = a.at(z=a.zh * 2 + 1 - a.zl)
        return remote(own, self.piece(a.x, a.y, a.zl), self.sz, self.rz, to)

    def x1(self, side):
        a = self.at
        ref = self.piece(a.x, a.y)
        to = a.x + 1 if side == 0 else a.x + 3
        return remote(ref, ref, self.sx.at[side], self.rx.at[side], a.at(x=to))

    def x2(self):
        a = self.at
        ref = self.piece(a.x - self.turn, a.y)
        return remote(ref, ref, self.sf, self.rf, a.at(x=a.x + self.turn + 4))

    def y1(self, side, t):
        a = self.at
        ref = self.piece(a.x + t, a.y)
        to = a.y + 1 if side == 0 else a.y + 3
        return remote(ref, ref, self.sy.at[side, t], self.ry.at[side, t], a.at(y=to))

    def y2(self, t):
        a = self.at
        ref = self.piece(a.x + t, a.y - self.turn)
        return remote(ref, ref, self.sg.at[t], self.rg.at[t], a.at(y=a.y + self.turn + 4))

    def c1(self, t):
        a = self.at
        ref = self.piece(a.x + t, 0, whole=True)
        return remote(ref, ref, self.sc.at[t], self.rc.at[t], a.at(core=1 - a.core))

    def start(self):
        self.z1().start()

    def along(self):
        self.z1().wait_recv()
        for side in (0, 1):
            self.x1(side).start()

    def far(self):
        for side in (0, 1):
            self.x1(side).wait_recv()
        self.x2().start()
        for t in (0, 1, 3):
            for side in (0, 1):
                self.y1(side, t).start()

    def last(self):
        self.x2().wait_recv()
        for side in (0, 1):
            self.y1(side, 2).start()

    def across(self):
        for t in (0, 1, 3, 2):
            for side in (0, 1):
                self.y1(side, t).wait_recv()
            self.y2(t).start()

    def share(self):
        for t in (0, 1, 3, 2):
            self.y2(t).wait_recv()
            self.c1(t).start()

    def ready(self):
        for t in range(4):
            self.c1(t).wait_recv()

    def drain(self):
        self.z1().wait_send()
        self.x2().wait_send()
        for side in (0, 1):
            self.x1(side).wait_send()
            for t in range(4):
                self.y1(side, t).wait_send()
        for t in range(4):
            self.y2(t).wait_send()
            self.c1(t).wait_send()


class Ring:
    def __init__(self, at, buf, sems):
        self.at, self.buf = at, buf
        self.half, self.width = buf.shape[0] // 2, buf.shape[1] // 4
        self.send, self.recv, self.relay_send = sems

    def view(self, place, half):
        column = pl.multiple_of((place + 4) % 4 * self.width, 128)
        return self.buf.at[pl.ds(half * self.half, self.half), pl.ds(column, self.width)]

    def copy(self, place, half, side, send):
        ref = self.view(place, half)
        to = self.at.z + 2 if side == 0 else self.at.z + 6
        return remote(ref, ref, send, self.recv.at[(place + 4) % 4, half], self.at.at(z=to))

    def out(self, side, half):
        return self.copy(self.at.zh, half, side, self.send.at[side, half])

    def forward(self, side):
        place = self.at.zh - 1 if side == 0 else self.at.zh + 1
        return self.copy(place, side, side, self.relay_send.at[side])

    def came(self, place, half):
        ref = self.view(place, half)
        pltpu.make_async_copy(ref, ref, self.recv.at[(place + 4) % 4, half]).wait()

    def start(self):
        for side, half in ((0, 0), (1, 1), (0, 1), (1, 0)):
            self.out(side, half).start()

    def relay(self):
        self.came(self.at.zh - 1, 0)
        self.forward(0).start()
        self.came(self.at.zh + 1, 1)
        self.forward(1).start()

    def ready(self):
        self.came(self.at.zh - 1, 1)
        self.came(self.at.zh + 1, 0)
        self.came(self.at.zh + 2, 0)
        self.came(self.at.zh + 2, 1)

    def drain(self):
        for side in (0, 1):
            for half in (0, 1):
                self.out(side, half).wait_send()
            self.forward(side).wait_send()


def bucket_rows(pick, table):
    first = table.astype(jnp.bfloat16)
    rest = table - first.astype(jnp.float32)
    second = rest.astype(jnp.bfloat16)
    third = (rest - second.astype(jnp.float32)).astype(jnp.bfloat16)
    terms = jnp.concatenate([first, second, third], axis=0)
    return jnp.dot(pick, terms, preferred_element_type=jnp.float32)


def block_kernel(
    tokens_in, ids_in, clips_in, shift_in, scale_in, gate_in, wq, wo, qg_in, kg_in, out,
    tokens, ids, their_ids, clips, shift, scale, gate, qg, kg, cosine, sine, mask, result, in_sem, out_sem, id_sem,
    wq_all, wo_all, raw, a1, a2, row_a, row_b, row_gate, stat_in, stat_col, stats,
    home1, mine1, theirs1, acc1,
    stat_send, stat_recv, c1_send, c1_recv,
    qs0, qs1, qs2, qs3, qs4, qs5, qs6, qs7, qs8,
    os0, os1, os2, os3, os4, os5, os6, os7, os8,
    as0, as1, bs0, bs1, bs2,
    fs0, fs1, fs2, fs3, fs4, fs5, fs6, fs7, fs8, fs9, fs10, fs11,
):
    at = Place()
    wide = tokens.shape[1]
    heads = qg.shape[0] // HD
    buckets = shift.shape[0]
    here = pl.ds(pl.multiple_of(at.zl * (2 * wide), 128), 2 * wide)
    loads = [
        pltpu.make_async_copy(src, dst, in_sem.at[i])
        for i, (src, dst) in enumerate(
            [
                (tokens_in, tokens), (ids_in, ids), (scale_in.at[:, here], scale),
                (shift_in.at[:, here], shift), (gate_in, gate), (clips_in, clips),
                (qg_in, qg), (kg_in, kg),
            ]
        )
    ]
    for load in loads:
        load.start()

    barrier = pltpu.get_barrier_semaphore()
    friends = [at.at(z=at.z + o) for o in range(1, 8)]
    friends += [at.at(x=at.x + 1), at.at(x=at.x + 3), at.at(y=at.y + 1), at.at(y=at.y + 3)]
    friends += [at.at(core=1 - at.core)]
    for friend in friends:
        pl.semaphore_signal(barrier, inc=1, device_id=friend, device_id_type=MESH)
    pl.semaphore_wait(barrier, len(friends))

    qkv = Weights(at, wq, wq_all, (qs0, qs1, qs2, qs3, qs4, qs5, qs6, qs7, qs8), False)
    proj = Weights(at, wo, wo_all, (os0, os1, os2, os3, os4, os5, os6, os7, os8), True, at.zl * 4 * wo.shape[0])
    one = Spread(at, tokens_in, raw, (as0, as1))
    two = Ring(at, a2, (bs0, bs1, bs2))
    other = Foreign(at, wo, wo_all, (fs0, fs1, fs2, fs3, fs4, fs5, fs6, fs7, fs8, fs9, fs10, fs11))

    partner = at.at(z=at.zh * 2 + 1 - at.zl)
    loads[1].wait()
    id_copy = remote(ids, their_ids, id_sem.at[0], id_sem.at[1], partner)
    id_copy.start()
    other.start()
    one.start()
    qkv.start()
    for i, load in enumerate(loads):
        if i != 1:
            load.wait()

    lane = lax.broadcasted_iota(jnp.int32, (16, HD), 1)

    @pl.loop(0, 8)
    def _(i):
        rows = pl.ds(pl.multiple_of(i * 16, 16), 16)
        part = tokens[rows, :].astype(jnp.float32)
        mean = jnp.sum(part, axis=1, keepdims=True) * (1.0 / wide)
        part = part - mean
        spread = jnp.sum(part * part, axis=1, keepdims=True)
        stat_in[rows, :] = jnp.where(lane == 0, mean, jnp.where(lane == 1, spread, 0.0))

    index = lax.broadcasted_iota(jnp.int32, (HD, HD), 0)
    lanes = lax.broadcasted_iota(jnp.int32, (HD, HD), 1)
    stats[at.z] = stat_in[...].T[0:8, :]

    def stat_copy(o):
        ref = stats.at[at.z]
        return remote(ref, ref, stat_send.at[o - 1], stat_recv.at[o - 1], at.at(z=at.z + o))

    for o in range(1, 8):
        stat_copy(o).start()

    qkv.near()
    one.relay((0,))
    count = clips.shape[1]
    lengths = jnp.broadcast_to(clips[...], (8, count)).astype(jnp.bfloat16)
    before = (
        lax.broadcasted_iota(jnp.int32, (count, count), 0)
        <= lax.broadcasted_iota(jnp.int32, (count, count), 1)
    ).astype(jnp.bfloat16)
    ends = jnp.dot(lengths, before, preferred_element_type=jnp.float32)[0:1, :]
    first = (at.zl * 4 + at.x) * 8 + at.y * 2 + at.core
    token = (first * HD + lax.broadcasted_iota(jnp.int32, (HD, count), 0)).astype(jnp.float32)
    passed = ends <= token
    clip = jnp.sum(jnp.where(passed, 1.0, 0.0), axis=1, keepdims=True)
    begin = jnp.sum(jnp.where(passed, clips[...].astype(jnp.float32), 0.0), axis=1, keepdims=True)
    clip = jnp.broadcast_to(clip, (HD, HD))
    mask[...] = jnp.where(clip == clip.T, 1.0, 0.0)
    half = HD // 2
    power = (lanes[:, 0:half]).astype(jnp.float32) * (-math.log(10000.0) / half)
    angles = (token[:, 0:1] - begin) * jnp.exp(power)
    cosine_half, sine_half = jnp.cos(angles), jnp.sin(angles)
    cosine[...] = jnp.concatenate([cosine_half, cosine_half], axis=1)
    sine[...] = jnp.concatenate([-sine_half, sine_half], axis=1)

    def bucket_rows_of(bucket, table):
        bucket = jnp.broadcast_to(bucket[...].astype(jnp.float32), (HD, HD)).T.astype(jnp.int32)
        pick = (bucket[:, 0 : 3 * buckets] == lanes[:, 0 : 3 * buckets] % buckets).astype(jnp.bfloat16)
        return bucket_rows(pick, table[...])

    row_a[at.zl] = 1.0 + bucket_rows_of(ids, scale)
    row_b[at.zl] = bucket_rows_of(ids, shift)
    row_gate[...] = bucket_rows_of(ids, gate)
    id_copy.wait()
    row_a[1 - at.zl] = 1.0 + bucket_rows_of(their_ids, scale)
    row_b[1 - at.zl] = bucket_rows_of(their_ids, shift)

    qkv.far()
    one.relay((1, 2))
    proj.start()
    qkv.across((3, 1))
    for o in range(1, 8):
        stat_copy(o).wait_recv()

    for block in (0, 1):
        parts = [stats[2 * c + block] for c in range(4)]
        mean = (parts[0][0:1] + parts[1][0:1] + parts[2][0:1] + parts[3][0:1]) * 0.25
        total = jnp.zeros_like(mean)
        for part in parts:
            apart = part[0:1] - mean
            total = total + part[1:2] + wide * (apart * apart)
        rstd = lax.rsqrt(total * (1.0 / (4 * wide)) + EPS)
        stat_col[block] = jnp.where(index == 0, mean, jnp.where(index == 1, rstd, 0.0)).T

    qkv.across((2,))
    other.along()
    for slot in range(4):
        one.ready((slot,))
        block, part = slot % 2, pl.ds(slot // 2 * wide, wide)

        @pl.loop(0, 8)
        def _(i):
            rows = pl.ds(pl.multiple_of(i * 16, 16), 16)
            normed = raw[block, rows, part].astype(jnp.float32) - stat_col[block, rows, 0:1]
            normed = normed * stat_col[block, rows, 1:2]
            a1[block, rows, part] = (normed * row_a[block, rows, part] + row_b[block, rows, part]).astype(
                jnp.bfloat16
            )

    qkv.ready()
    other.far()

    pieces, piece = result.shape[0], result.shape[2]
    own_rows = pl.ds(pl.multiple_of(at.zl * HD, HD), HD)
    other_rows = pl.ds(pl.multiple_of((1 - at.zl) * HD, HD), HD)

    def swap1(h):
        return remote(mine1.at[h], theirs1.at[h], c1_send.at[h], c1_recv.at[h], partner)

    def store(n):
        columns = pl.ds(pl.multiple_of(n * piece, HD), piece)
        return pltpu.make_async_copy(result.at[n], out.at[:, columns], out_sem.at[n])

    @pl.loop(0, heads)
    def _(h):
        columns = pl.ds(pl.multiple_of(h * (3 * HD), HD), 3 * HD)
        mine1[h] = jnp.dot(
            a1[1 - at.zl], wq_all[:, columns], preferred_element_type=jnp.float32
        ).astype(jnp.bfloat16)
        swap1(h).start()

    @pl.loop(0, heads)
    def _(h):
        columns = pl.ds(pl.multiple_of(h * (3 * HD), HD), 3 * HD)
        home1[h] = jnp.dot(a1[at.zl], wq_all[:, columns], preferred_element_type=jnp.float32)

    proj.near()
    other.last()

    def rotate(vectors, gains):
        power = jnp.mean(vectors * vectors, axis=-1, keepdims=True)
        vectors = vectors * lax.rsqrt(power + EPS) * gains
        turned = pltpu.roll(vectors, HD // 2, axis=1)
        return (vectors * cosine[...] + turned * sine[...]).astype(jnp.bfloat16)

    @pl.loop(0, heads)
    def _(h):
        swap1(h).wait_recv()
        head = pl.ds(pl.multiple_of(h * HD, HD), HD)
        joined = home1[h] + theirs1[h].astype(jnp.float32)
        query = rotate(joined[:, 0:HD], qg[head].reshape(1, HD))
        key = rotate(joined[:, HD : 2 * HD], kg[head].reshape(1, HD))
        value = joined[:, 2 * HD : 3 * HD].astype(jnp.bfloat16)
        scores = lax.dot_general(
            query, key, (((1,), (1,)), ((), ())), preferred_element_type=jnp.float32
        ) * (1.0 / math.sqrt(HD))
        raised = jnp.where(mask[...] > 0.0, jnp.exp(scores), 0.0)
        weights = (raised / jnp.sum(raised, axis=-1, keepdims=True)).astype(jnp.bfloat16)
        spot = pl.ds(pl.multiple_of(at.zh * (heads * HD) + h * HD, HD), HD)
        a2[:, spot] = jnp.dot(weights, value, preferred_element_type=jnp.float32).astype(
            jnp.bfloat16
        )

    two.start()
    proj.far()
    other.across()
    two.relay()
    proj.across()
    other.share()
    proj.ready()
    other.ready()
    two.ready()

    @pl.loop(0, pieces)
    def _(n):
        columns = pl.ds(pl.multiple_of(n * piece, HD), piece)
        projected = jnp.dot(a2[...], wo_all[:, columns], preferred_element_type=jnp.float32)
        result[n] = (row_gate[:, columns] * projected).astype(jnp.bfloat16)
        store(n).start()

    qkv.drain()
    proj.drain()
    one.drain()
    two.drain()
    other.drain()
    for o in range(1, 8):
        stat_copy(o).wait_send()

    @pl.loop(0, heads)
    def _(h):
        swap1(h).wait_send()

    @pl.loop(0, pieces)
    def _(n):
        store(n).wait()


def shards(
    tokens, bucket_ids, clip_lengths, shift_table, scale_table, gate_table, w_qkv, q_gain, k_gain, w_out
):
    rows, wide = tokens.shape
    heads = w_qkv.shape[1] // (3 * HD)
    pieces = 5
    piece = wide // pieces
    bf16, f32 = jnp.bfloat16, jnp.float32
    dma = pltpu.SemaphoreType.DMA
    weight_sems = [dma((2, 2)), dma((2, 2)), dma((2,)), dma((2,)), dma((3, 2)), dma((3, 2)), dma((3, 4)), dma((3, 4)), dma]
    ring_sems = [dma((2, 2)), dma((4, 2)), dma((2,))]
    foreign_sems = [dma, dma, dma((2,)), dma((2,)), dma, dma, dma((2, 4)), dma((2, 4))] + [dma((4,))] * 4
    spread_sems = [dma((10,)), dma((4, 2))]
    hbm = pl.BlockSpec(memory_space=pltpu.HBM)
    return pl.pallas_call(
        block_kernel,
        out_shape=jax.ShapeDtypeStruct((rows, wide), bf16),
        in_specs=[hbm] * 10,
        out_specs=hbm,
        scratch_shapes=[
            pltpu.VMEM((rows, wide), bf16),
            pltpu.VMEM((1, rows), jnp.int32),
            pltpu.VMEM((1, rows), jnp.int32),
            pltpu.VMEM((1, clip_lengths.shape[0]), jnp.int32),
            pltpu.VMEM((shift_table.shape[0], 2 * wide), f32),
            pltpu.VMEM((shift_table.shape[0], 2 * wide), f32),
            pltpu.VMEM((shift_table.shape[0], wide), f32),
            pltpu.VMEM((heads * HD,), f32),
            pltpu.VMEM((heads * HD,), f32),
            pltpu.VMEM((rows, HD), f32),
            pltpu.VMEM((rows, HD), f32),
            pltpu.VMEM((rows, rows), f32),
            pltpu.VMEM((pieces, rows, piece), bf16),
            dma((8,)),
            dma((pieces,)),
            dma((2,)),
            pltpu.VMEM((4 * w_qkv.shape[0], w_qkv.shape[1]), bf16),
            pltpu.VMEM((8 * w_out.shape[0], w_out.shape[1]), bf16),
            pltpu.VMEM((2, rows, 2 * wide), bf16),
            pltpu.VMEM((2, rows, 2 * wide), bf16),
            pltpu.VMEM((rows, 4 * heads * HD), bf16),
            pltpu.VMEM((2, rows, 2 * wide), f32),
            pltpu.VMEM((2, rows, 2 * wide), f32),
            pltpu.VMEM((rows, wide), f32),
            pltpu.VMEM((rows, HD), f32),
            pltpu.VMEM((2, rows, HD), f32),
            pltpu.VMEM((8, 8, rows), f32),
            pltpu.VMEM((heads, rows, 3 * HD), f32),
            pltpu.VMEM((heads, rows, 3 * HD), bf16),
            pltpu.VMEM((heads, rows, 3 * HD), bf16),
            pltpu.VMEM((2 * rows, 3 * HD), f32),
            dma((7,)), dma((7,)),
            dma((heads,)), dma((heads,)),
        ]
        + weight_sems + weight_sems + spread_sems + ring_sems + foreign_sems,
        compiler_params=pltpu.CompilerParams(
            collective_id=0, has_side_effects=True, vmem_limit_bytes=60 * 1024 * 1024
        ),
    )(
        tokens, bucket_ids.reshape(1, rows), clip_lengths.reshape(1, -1), shift_table, scale_table, gate_table,
        w_qkv, w_out, q_gain, k_gain,
    )


def solution(mesh):
    in_specs = (
        P(("row", "depth"), "col"),
        P(("row", "depth")),
        P(),
        P(),
        P(),
        P(None, "col"),
        P("row", "col"),
        P("col"),
        P("col"),
        P("row", "col"),
    )
    out_specs = P(("row", "depth"), "col")
    return jax.shard_map(shards, mesh=mesh, in_specs=in_specs, out_specs=out_specs, check_vma=False)
```
